256 devices in a mesh: group: 2 (over y_lo), slab: 32 (over y_hi, z, core), tile: 4 (over x).
Axes of the slice: x: 4, y: 4 (y_hi: 2, y_lo: 2; y = y_hi * 2 + y_lo), z: 8, core: 2. Of those that a mesh axis runs over, the one named last changes fastest.
Arguments:
- populations: float32 [2, 19, 256, 32, 128], P('group', None, 'slab', 'tile'), may hold values from 0 to 1, as said below
- fluid: int32 [2, 256, 32, 128], P('group', 'slab', 'tile'), may hold values 0 or 1
- couple: int32 [2, 64, 4, 1024], P('group', 'slab', 'tile'), may hold values from 0 to 8191, as said below
- owner: int32 [1024, 1], P(('group', 'slab', 'tile')), may hold values from 0 to 3; in each aligned block of 4 rows (0 to 3, 4 to 7, ...) at most 2 rows name the same one
- vertex_site: int32 [1024, 642], P(('group', 'slab', 'tile')), may hold values from 0 to 7038, as said below
- frac: float32 [1024, 3, 642], P(('group', 'slab', 'tile')), may hold values from 0 to 1
- ref_shape: float32 [1024, 3, 642], P(('group', 'slab', 'tile')), may hold values from -8 to 8
Outputs:
- populations_new: float32 [2, 19, 256, 32, 128], P('group', None, 'slab', 'tile')
- vertex_velocity: float32 [1024, 3, 642], P(('group', 'slab', 'tile'))
The draws below stay inside these ranges and needn't reach their ends.
Inputs may be any that keep to these rules, and one draw needn't show every extreme that they name: `populations`: every population is positive. Within one block (fixed group g, slab s, tile t) the 2048 entries couple[g, 2s, t] and couple[g, 2s+1, t] are distinct local sites. `owner`: among the 4 cells of one device at most 2 name the same tile, and in every draw some tile is named by exactly 2 of some device's cells. `vertex_site`: each site's coordinates are at most 6, 6 and 126 within the block.
All inputs are finite; a program needn't handle non-finite values. No bound on the sum of `fluid` on one device may be relied on, other than what follows from the above.
Results may differ from the reference program's by a relative error of at most 0.0005.
Values sent between devices are 32-bit elements; how exact they have to be, the bound alone decides.
A program may use at most 128 MiB of HBM per device.

```python
import math
import jax
import jax.numpy as jnp
import numpy as np

CX = 8
CY = 8
NZ = 128
VERTS = 642
CELL_DEV = 4
EDGE = 1024
CAP = 2
NX = 256
NY = 32
SITES = 8192
CELLS = 1024
N_SLAB = 32
N_TILE = 4


lattice_c = [(0, 0, 0), (1, 0, 0), (-1, 0, 0), (0, 1, 0), (0, -1, 0), (0, 0, 1), (0, 0, -1), (1, 1, 0), (-1, -1, 0), (1, -1, 0), (-1, 1, 0), (1, 0, 1), (-1, 0, -1), (1, 0, -1), (-1, 0, 1), (0, 1, 1), (0, -1, -1), (0, 1, -1), (0, -1, 1)]


lattice_w = [1.0 / 3.0] + [1.0 / 18.0] * 6 + [1.0 / 36.0] * 12


def draw_populations(key, part):
    key = jax.random.fold_in(key, 11)
    key_density, key_flow, key_noise = jax.random.split(key, 3)
    grid_shape = (2, NX, NY, NZ)
    density = jax.random.uniform(key_density, grid_shape, jnp.float32, 0.9, 1.1)
    flow = jax.random.uniform(key_flow, (3,) + grid_shape, jnp.float32, -0.08, 0.08)
    noise = jax.random.uniform(key_noise, (19,) + grid_shape, jnp.float32, -0.15, 0.15)
    terms = []
    for i in range(19):
        along = float(lattice_c[i][0]) * flow[0] + float(lattice_c[i][1]) * flow[1] + float(lattice_c[i][2]) * flow[2]
        terms.append(lattice_w[i] * density * (1.0 + 3.0 * along + noise[i]))
    return jnp.stack(terms, axis=1)


def draw_couple(key, part):
    key = jax.random.fold_in(key, 12)
    key_list = jax.random.split(key, 2 * N_SLAB * N_TILE)
    chosen = jax.vmap(lambda single: jax.random.permutation(single, SITES)[:2 * EDGE])(key_list)
    chosen = chosen.reshape(2, N_SLAB, N_TILE, 2, EDGE).transpose(0, 1, 3, 2, 4)
    return chosen.reshape(2, 2 * N_SLAB, N_TILE, EDGE).astype(jnp.int32)


def draw_vertex_site(key, part):
    key = jax.random.fold_in(key, 13)
    key_centre, key_offset = jax.random.split(key)
    limits = jnp.array([CX - 4, CY - 4, NZ - 4], jnp.int32)
    centre = jax.random.randint(key_centre, (CELLS, 3, 1), 3, limits[None, :, None])
    offset = jax.random.randint(key_offset, (CELLS, 3, VERTS), -3, 4)
    point = centre + offset
    return (point[:, 0] * (CY * NZ) + point[:, 1] * NZ + point[:, 2]).astype(jnp.int32)


def with_ends(values, rng, smallest, largest):
    dims = values.shape
    index_at = [jax.random.randint(jax.random.fold_in(rng, axis), (), 0, dims[axis]) for axis in range(len(dims))]
    values = values.at[tuple(index_at)].set(smallest)
    longest = dims.index(max(dims))
    index_at[longest] = (index_at[longest] + 1) % dims[longest]
    return values.at[tuple(index_at)].set(largest)


def level_of(own_key, dims, shards, low, high):
    def one(dim, shards_of):
        steps = jax.random.uniform(jax.random.fold_in(jax.random.fold_in(own_key, 6), dim), (shards_of,), jnp.float32, low / len(shards), high / len(shards))
        return jnp.repeat(jnp.exp(steps), dims[dim] // shards_of).reshape((-1,) + (1,) * (len(dims) - dim - 1))

    loudness = one(*shards[0])
    for cut in shards[1:]:
        loudness = loudness * one(*cut)
    return loudness


def routed_block(rng, own, number, rows, number_of, top, most, lean):
    sequence = jax.random.permutation(rng, number_of)
    crowded, usual = portions_of(number_of, rows * top, most, lean, True), portions_of(number_of, rows * top, most, lean, False)
    places = jnp.arange(number_of)

    def named(tallies, rotation):
        used = int((tallies > 0).sum())
        fixed = max(1, used // 4)
        moved = fixed + (places - fixed + rotation * (used - fixed)) % max(1, number_of - fixed)
        return jnp.zeros((number_of,), jnp.int32).at[sequence[jnp.where(places < fixed, places, moved)]].set(jnp.asarray(tallies, jnp.int32))

    tallies = jnp.where(number % 4 == 0, named(crowded, number // 4), named(usual, number - number // 4 - 1))
    mixed = jax.random.permutation(jax.random.fold_in(own, 3), number_of)
    donor, sink = mixed[0:number_of // 2 * 2:2], mixed[1:number_of // 2 * 2:2]
    margin = jnp.minimum(tallies[donor] - 1, most - tallies[sink]) // 2
    margin = jnp.where((donor == sequence[0]) | (sink == sequence[0]) | (tallies[sink] == 0), 0, jnp.maximum(margin, 0))
    moved = jax.random.randint(jax.random.fold_in(own, 4), (number_of // 2,), 0, 1 << 20) % (margin + 1)
    tallies = tallies.at[donor].add(-moved).at[sink].add(moved)
    labels = jnp.searchsorted(jnp.cumsum(tallies), jnp.arange(rows * top), side="right").astype(jnp.int32)
    grid = labels.reshape(top, rows).T
    grid = grid[jax.random.permutation(jax.random.fold_in(own, 1), rows)]
    rotation = jax.random.randint(jax.random.fold_in(own, 2), (rows, 1), 0, top)
    return jnp.take_along_axis(grid, (jnp.arange(top)[None, :] + rotation) % top, axis=1)


def portions_of(amount, total, reach, slope, full):
    portions = [(1 << 20) // math.isqrt(grade ** slope) + 1 for grade in range(1, amount + 1)]
    largest = reach if full else min(reach, max(-(-total // amount), total * portions[0] // sum(portions)))
    least = 1 if total - largest >= amount - 1 else 0
    holding, surplus = [largest] + [least] * (amount - 1), total - largest - least * (amount - 1)
    while surplus > 0:
        movable = [i for i in range(1, amount) if holding[i] < largest] or [i for i in range(1, amount) if holding[i] < reach]
        pool, budget = sum([portions[i] for i in movable]), surplus
        for i in movable:
            extra = min(reach - holding[i], max(1, budget * portions[i] // pool), surplus)
            holding[i] = holding[i] + extra
            surplus = surplus - extra
    return np.array(holding)


def scatter_about(rng, extent, width, limit, pieces=(), held_as=jnp.bfloat16):
    drawn = jax.random.normal(rng, extent, jnp.float32) * width
    if len(pieces) > 0:
        drawn = level_of(rng, extent, pieces, -0.22, 0.18) * drawn
    return jnp.clip(drawn, min=-limit, max=limit).astype(held_as)


def setup_inputs(seed: int = 0) -> dict:
    keys = jax.random.split(jax.random.key(seed), 8)
    populations = draw_populations(jax.random.fold_in(keys[7], 71), 0)
    fluid = with_ends((jax.random.randint(keys[1], (2, NX, NY, NZ), 0, 10) < 9).astype(jnp.int32), jax.random.fold_in(keys[1], 1), 0, 1)
    couple = draw_couple(jax.random.fold_in(keys[7], 71), 0)
    owner_keys = jax.random.split(jax.random.fold_in(keys[3], 1), CELLS // CELL_DEV)
    owner_turns = jax.random.permutation(jax.random.fold_in(keys[3], 3), CELLS // CELL_DEV)
    owner = jax.vmap(lambda own, number: routed_block(jax.random.fold_in(keys[3], 2), own, number, CELL_DEV, N_TILE, 1, CAP, 2))(owner_keys, owner_turns).reshape((CELLS, 1))
    vertex_site = draw_vertex_site(jax.random.fold_in(keys[7], 71), 0)
    frac = jnp.clip(1.0 * jax.random.uniform(keys[5], (CELLS, 3, VERTS), jnp.float32) ** level_of(keys[5], (CELLS, 3, VERTS), ((0, 256),), -0.2, 0.2), 0.0, 1.0)
    ref_shape = scatter_about(keys[6], (CELLS, 3, VERTS), 2.0, 8.0, ((0, 256),), jnp.float32)
    return dict(populations=populations, fluid=fluid, couple=couple, owner=owner, vertex_site=vertex_site, frac=frac, ref_shape=ref_shape)


lattice_c = [(0, 0, 0), (1, 0, 0), (-1, 0, 0), (0, 1, 0), (0, -1, 0), (0, 0, 1), (0, 0, -1), (1, 1, 0), (-1, -1, 0), (1, -1, 0), (-1, 1, 0), (1, 0, 1), (-1, 0, -1), (1, 0, -1), (-1, 0, 1), (0, 1, 1), (0, -1, -1), (0, 1, -1), (0, -1, 1)]
lattice_w = [1.0 / 3.0] + [1.0 / 18.0] * 6 + [1.0 / 36.0] * 12
opposite = [0, 2, 1, 4, 3, 6, 5, 8, 7, 10, 9, 12, 11, 14, 13, 16, 15, 18, 17]
tau_coarse = 0.8
tau_fine = 1.1
stiffness = 0.01


def moments(popul):
    density = popul[0]
    momenta = [jnp.zeros_like(density), jnp.zeros_like(density), jnp.zeros_like(density)]
    for i in range(1, 19):
        density = density + popul[i]
        for d in range(3):
            if lattice_c[i][d] != 0:
                momenta[d] = momenta[d] + float(lattice_c[i][d]) * popul[i]
    return density, momenta


def equilibrium(density, velocity):
    speed_sq = velocity[0] * velocity[0] + velocity[1] * velocity[1] + velocity[2] * velocity[2]
    terms = []
    for i in range(19):
        along = float(lattice_c[i][0]) * velocity[0] + float(lattice_c[i][1]) * velocity[1] + float(lattice_c[i][2]) * velocity[2]
        terms.append(lattice_w[i] * density * (1.0 + 3.0 * along + 4.5 * along * along - 1.5 * speed_sq))
    return jnp.stack(terms)


def rescale(values, factor):
    density, momenta = moments(values)
    target = equilibrium(density, [momenta[d] / density for d in range(3)])
    return target + factor * (values - target)


def collide(popul, force, relax, fluid_mask):
    density, momenta = moments(popul)
    velocity = [(momenta[d] + relax * force[d]) / density for d in range(3)]
    target = equilibrium(density, velocity)
    relaxed = popul - (popul - target) / relax
    return jnp.where(fluid_mask > 0, relaxed, popul)


def stream(relaxed, padded, fluid_mask, wet_padded):
    size_x, size_y, size_z = relaxed.shape[1:]
    moved = []
    for i in range(19):
        a, b, e = lattice_c[i]
        source = padded[i, 1 - a:1 - a + size_x, 1 - b:1 - b + size_y, 1 - e:1 - e + size_z]
        open_side = wet_padded[1 - a:1 - a + size_x, 1 - b:1 - b + size_y, 1 - e:1 - e + size_z]
        moved.append(jnp.where(open_side > 0, source, relaxed[opposite[i]]))
    return jnp.where(fluid_mask > 0, jnp.stack(moved), relaxed)


def sweep(lattice, force, relax, fluid_mask):
    relaxed = collide(lattice, force, relax, fluid_mask)
    padded = jnp.pad(relaxed, ((0, 0), (1, 1), (1, 1), (1, 1)))
    wet_padded = jnp.pad(fluid_mask, 1)
    return stream(relaxed, padded, fluid_mask, wet_padded)


def corner_terms(placed):
    frac_x, frac_y, frac_z = placed[:, 0], placed[:, 1], placed[:, 2]
    result = []
    for a in (0, 1):
        for b in (0, 1):
            for e in (0, 1):
                weight = (frac_x if a else 1.0 - frac_x) * (frac_y if b else 1.0 - frac_y) * (frac_z if e else 1.0 - frac_z)
                result.append((a * CY * NZ + b * NZ + e, weight))
    return result


def membrane(vertex_site, frac, ref_shape):
    pos_x = (vertex_site // (CY * NZ)).astype(jnp.float32) + frac[:, 0]
    pos_y = ((vertex_site // NZ) % CY).astype(jnp.float32) + frac[:, 1]
    pos_z = (vertex_site % NZ).astype(jnp.float32) + frac[:, 2]
    position = jnp.stack([pos_x, pos_y, pos_z], axis=1)
    centre = jnp.mean(position, axis=2, keepdims=True)
    return -stiffness * (position - centre - ref_shape)


def to_blocks(field):
    lead = field.shape[:-3]
    shaped = field.reshape(lead + (N_SLAB, CX, N_TILE, CY, NZ))
    shaped = jnp.moveaxis(shaped, -3, -4)
    return shaped.reshape(lead + (N_SLAB, N_TILE, CX * CY * NZ))


def from_blocks(blocks):
    lead = blocks.shape[:-3]
    shaped = blocks.reshape(lead + (N_SLAB, N_TILE, CX, CY, NZ))
    shaped = jnp.moveaxis(shaped, -4, -3)
    return shaped.reshape(lead + (N_SLAB * CX, N_TILE * CY, NZ))


def reading(lattice, force_field, start, corners):
    density, momenta = moments(lattice)
    velocity = jnp.stack([(momenta[d] + 0.5 * force_field[d]) / density for d in range(3)])
    vel_flat = to_blocks(velocity).reshape(3, -1)
    total = None
    for offset, weight in corners:
        term = weight[None] * vel_flat[:, start + offset]
        total = term if total is None else total + term
    return total


def reference(populations, fluid, couple, owner, vertex_site, frac, ref_shape):
    block_count = N_SLAB * N_TILE
    site_count = CX * CY * NZ
    lists = couple.reshape(2, N_SLAB, 2, N_TILE, EDGE)
    offsets = (jnp.arange(block_count, dtype=jnp.int32) * site_count)[:, None]
    bulk_read = (offsets + lists[0, :, 0].reshape(block_count, EDGE)).reshape(-1)
    bulk_write = (offsets + lists[0, :, 1].reshape(block_count, EDGE)).reshape(-1)
    window_write = (offsets + lists[1, :, 0].reshape(block_count, EDGE)).reshape(-1)
    window_read = (offsets + lists[1, :, 1].reshape(block_count, EDGE)).reshape(-1)
    bulk_flat = to_blocks(populations[0]).reshape(19, -1)
    window_flat = to_blocks(populations[1]).reshape(19, -1)
    from_bulk = bulk_flat[:, bulk_read]
    from_window = window_flat[:, window_read]
    window_flat = window_flat.at[:, window_write].set(rescale(from_bulk, tau_fine / (2.0 * tau_coarse)))
    bulk_flat = bulk_flat.at[:, bulk_write].set(rescale(from_window, 2.0 * tau_coarse / tau_fine))

    push = membrane(vertex_site, frac, ref_shape)
    holder = jnp.arange(CELLS, dtype=jnp.int32) // CELL_DEV
    slab_of = (holder // N_TILE) % N_SLAB
    block_of = slab_of * N_TILE + owner[:, 0]
    start = (block_of * site_count)[:, None] + vertex_site
    corners = corner_terms(frac)
    force_flat = jnp.zeros((3, block_count * site_count), jnp.float32)
    for offset, weight in corners:
        force_flat = force_flat.at[:, (start + offset).reshape(-1)].add(jnp.moveaxis(weight[:, None, :] * push, 1, 0).reshape(3, -1))
    force_field = from_blocks(force_flat.reshape(3, N_SLAB, N_TILE, site_count))

    bulk = from_blocks(bulk_flat.reshape(19, N_SLAB, N_TILE, site_count))
    window_lat = from_blocks(window_flat.reshape(19, N_SLAB, N_TILE, site_count))
    bulk = sweep(bulk, force_field, tau_coarse, fluid[0])
    window_lat = sweep(window_lat, force_field, tau_fine, fluid[1])
    window_lat = sweep(window_lat, force_field, tau_fine, fluid[1])

    bulk_read_out = reading(bulk, force_field, start, corners)
    window_read_out = reading(window_lat, force_field, start, corners)
    total = 0.5 * (bulk_read_out + window_read_out)
    return jnp.stack([bulk, window_lat]), jnp.moveaxis(total, 0, 1)
```

```python
import jax
import jax.numpy as jnp
from jax import lax
from jax.experimental import pallas as pl
from jax.experimental.pallas import tpu as pltpu
from jax.sharding import PartitionSpec as P

MESH = pl.DeviceIdType.MESH
CX = 8
CY = 8
NZ = 128
XY = CX * CY
VERTS = 642
PAD = 768
CELLS = 4
CAP = 2
EDGE = 1024
TILES = 4

lattice_c = [
    (0, 0, 0),
    (1, 0, 0),
    (-1, 0, 0),
    (0, 1, 0),
    (0, -1, 0),
    (0, 0, 1),
    (0, 0, -1),
    (1, 1, 0),
    (-1, -1, 0),
    (1, -1, 0),
    (-1, 1, 0),
    (1, 0, 1),
    (-1, 0, -1),
    (1, 0, -1),
    (-1, 0, 1),
    (0, 1, 1),
    (0, -1, -1),
    (0, 1, -1),
    (0, -1, 1),
]
lattice_w = [1.0 / 3.0] + [1.0 / 18.0] * 6 + [1.0 / 36.0] * 12
opposite = [0, 2, 1, 4, 3, 6, 5, 8, 7, 10, 9, 12, 11, 14, 13, 16, 15, 18, 17]
tau_coarse = 0.8
tau_fine = 1.1
stiffness = 0.01

X_UP = [i for i in range(19) if lattice_c[i][0] == 1]
X_DOWN = [i for i in range(19) if lattice_c[i][0] == -1]
Y_UP = [i for i in range(19) if lattice_c[i][1] == 1]
Y_DOWN = [i for i in range(19) if lattice_c[i][1] == -1]
DIAGONAL = [7, 8, 9, 10]


def f32(x):
    return x.astype(jnp.float32)


def halves(x):
    high = x.astype(jnp.bfloat16)
    low = (x - f32(high)).astype(jnp.bfloat16)
    return high, low


def dot_nn(a, b):
    return lax.dot_general(a, b, (((1,), (0,)), ((), ())), preferred_element_type=jnp.float32)


def dot_nt(a, b):
    return lax.dot_general(a, b, (((1,), (1,)), ((), ())), preferred_element_type=jnp.float32)


def moments(popul):
    density = popul[0]
    momenta = [None, None, None]
    for i in range(1, 19):
        density = density + popul[i]
        for d in range(3):
            sign = lattice_c[i][d]
            if sign == 0:
                continue
            if momenta[d] is None:
                momenta[d] = popul[i]
            elif sign > 0:
                momenta[d] = momenta[d] + popul[i]
            else:
                momenta[d] = momenta[d] - popul[i]
    return density, momenta


def equilibrium(density, velocity):
    ux, uy, uz = velocity
    base = 1.0 - 1.5 * (ux * ux + uy * uy + uz * uz)
    terms = [None] * 19
    terms[0] = lattice_w[0] * density * base
    for i in range(1, 19, 2):
        along = None
        for d in range(3):
            sign = lattice_c[i][d]
            if sign == 0:
                continue
            if along is None:
                along = velocity[d]
            elif sign > 0:
                along = along + velocity[d]
            else:
                along = along - velocity[d]
        weight = lattice_w[i] * density
        even = base + 4.5 * along * along
        odd = 3.0 * along
        terms[i] = weight * (even + odd)
        terms[i + 1] = weight * (even - odd)
    return terms


def kernel(
    pop_hbm,
    fluid_hbm,
    couple_hbm,
    owner_ref,
    site_hbm,
    frac_hbm,
    shape_hbm,
    out_pop,
    out_vel,
    lat,
    fluid,
    couple,
    site,
    frac,
    rest,
    payload,
    cell_send,
    cell_recv,
    pop_half,
    edge_send,
    edge_recv,
    edge_high,
    edge_low,
    hat_xy,
    hat_z,
    force_send,
    force_recv,
    force,
    post,
    wet,
    open_mask,
    face_send,
    face_recv,
    row_send,
    row_recv,
    vel_send,
    vel_recv,
    ret_send,
    ret_recv,
    mine,
    in_sem,
    out_sem,
    cell_sems,
    pair_sems,
    face_sems,
    row_sems,
    ret_sems,
):
    g = lax.axis_index("group")
    s = lax.axis_index("slab")
    t = lax.axis_index("tile")
    slabs = lax.axis_size("slab")
    window = g == 1
    up_s, down_s = lax.rem(s + 1, slabs), lax.rem(s + slabs - 1, slabs)
    tile_at = [lax.rem(t + j, TILES) for j in range(TILES)]
    up_t, down_t = tile_at[1], tile_at[3]
    other = 1 - g

    loads = [
        pltpu.make_async_copy(src, dst, in_sem.at[k])
        for k, (src, dst) in enumerate(
            [
                (site_hbm, site),
                (frac_hbm, frac),
                (shape_hbm, rest),
                (couple_hbm, couple),
                (pop_hbm.at[0], lat),
                (fluid_hbm.at[0], fluid),
            ]
        )
    ]
    for load in loads:
        load.start()

    barrier = pltpu.get_barrier_semaphore()
    friends = [
        (other, s, t),
        (g, s, up_t),
        (g, s, down_t),
        (g, s, tile_at[2]),
        (g, up_s, t),
        (g, down_s, t),
        (g, up_s, up_t),
        (g, up_s, down_t),
        (g, down_s, up_t),
        (g, down_s, down_t),
    ]
    for friend in friends:
        pl.semaphore_signal(barrier, inc=1, device_id=friend, device_id_type=MESH)

    payload[...] = jnp.zeros_like(payload)
    for load in loads[:3]:
        load.wait()
    site_value = site[...]
    coords = [
        site_value >> 10,
        (site_value >> 7) & (CY - 1),
        site_value & (NZ - 1),
    ]
    for d in range(3):
        offset = frac[d]
        position = f32(coords[d]) + offset
        centre = jnp.sum(position, axis=1, keepdims=True) * (1.0 / VERTS)
        push = -stiffness * (position - centre - rest[d])
        for c in range(CELLS):
            payload[c, d : d + 1, 0:VERTS] = push[c : c + 1]
            payload[c, 3 + d : 4 + d, 0:VERTS] = offset[c : c + 1]
    for c in range(CELLS):
        payload[c, 6:7, 0:VERTS] = f32(site_value[c : c + 1])

    owners = [owner_ref[c] for c in range(CELLS)]
    ranks = []
    for c in range(CELLS):
        rank = jnp.int32(0)
        for before in range(c):
            rank = rank + jnp.where(owners[before] == owners[c], 1, 0)
        ranks.append(rank)

    def chosen(j, k, c):
        return jnp.where((owners[c] == tile_at[j]) & (ranks[c] == k), 1.0, 0.0)

    for j in range(TILES):
        for k in range(CAP):
            slot = chosen(j, k, 0) * payload[0]
            for c in range(1, CELLS):
                slot = slot + chosen(j, k, c) * payload[c]
            if j == 0:
                cell_recv[0, k] = slot
            else:
                cell_send[j, k] = slot

    pl.semaphore_wait(barrier, len(friends))

    cell_copies = [None] + [
        pltpu.make_async_remote_copy(
            src_ref=cell_send.at[j],
            dst_ref=cell_recv.at[j],
            send_sem=cell_sems.at[0, j],
            recv_sem=cell_sems.at[1, j],
            device_id=(g, s, tile_at[j]),
            device_id_type=MESH,
        )
        for j in range(1, TILES)
    ]
    for j in (2, 1, 3):
        cell_copies[j].start()

    def to_pair(src, dst, k):
        return pltpu.make_async_remote_copy(
            src_ref=src,
            dst_ref=dst,
            send_sem=pair_sems.at[0, k],
            recv_sem=pair_sems.at[1, k],
            device_id=(other, s, t),
            device_id_type=MESH,
        )

    loads[3].wait()
    loads[4].wait()
    row_0, row_1 = couple[0], couple[1]
    read_sites = row_0 + g * (row_1 - row_0)
    write_sites = row_1 + g * (row_0 - row_1)
    high, low = halves(lat[...].reshape(19 * XY, NZ))
    pop_half[:, 0:NZ] = high
    pop_half[:, NZ : 2 * NZ] = low
    chunk = 256
    for k in range(EDGE // chunk):
        sites = read_sites[:, k * chunk : (k + 1) * chunk]
        z_rows = lax.broadcasted_iota(jnp.int32, (NZ, chunk), 0)
        pick_z = jnp.where(z_rows == (sites & (NZ - 1)), 1.0, 0.0).astype(jnp.bfloat16)
        pick_z = jnp.concatenate([pick_z, pick_z], axis=0)
        xy_rows = lax.broadcasted_iota(jnp.int32, (XY, chunk), 0)
        pick_xy = jnp.where(xy_rows == (sites >> 7), 1.0, 0.0)
        found = dot_nn(pop_half[...], pick_z)
        for i in range(19):
            edge_send[i : i + 1, k * chunk : (k + 1) * chunk] = jnp.sum(
                found[i * XY : (i + 1) * XY] * pick_xy, axis=0, keepdims=True
            )
    rows = [edge_send[i : i + 1, :] for i in range(19)]
    density, momenta = moments(rows)
    target = equilibrium(density, [m / density for m in momenta])
    factor = jnp.where(window, 2.0 * tau_coarse / tau_fine, tau_fine / (2.0 * tau_coarse))
    for i in range(19):
        edge_send[i : i + 1, :] = target[i] + factor * (rows[i] - target[i])
    edge_copy = to_pair(edge_send, edge_recv, 0)
    edge_copy.start()

    total = None
    for j in (0, 1, 3, 2):
        if j > 0:
            cell_copies[j].wait_recv()
        for k in range(CAP):
            n = j * CAP + k
            cell = cell_recv[j, k]
            where_at = cell[6:7].astype(jnp.int32)
            z_rows = lax.broadcasted_iota(jnp.int32, (NZ, PAD), 0) - (where_at & (NZ - 1))
            frac_z = cell[5:6]
            weight_z = jnp.where(z_rows == 0, 1.0 - frac_z, jnp.where(z_rows == 1, frac_z, 0.0))
            z_high, z_low = halves(weight_z)
            hat_z[n, 0:NZ] = z_high
            hat_z[n, NZ : 2 * NZ] = z_low
            y_rows = lax.broadcasted_iota(jnp.int32, (CY, PAD), 0) - ((where_at >> 7) & (CY - 1))
            frac_y = cell[4:5]
            weight_y = jnp.where(y_rows == 0, 1.0 - frac_y, jnp.where(y_rows == 1, frac_y, 0.0))
            x_rows = lax.broadcasted_iota(jnp.int32, (CX, PAD), 0) - (where_at >> 10)
            frac_x = cell[3:4]
            weight_x = jnp.where(x_rows == 0, 1.0 - frac_x, jnp.where(x_rows == 1, frac_x, 0.0))
            for x in range(CX):
                hat_xy[n, x * CY : (x + 1) * CY] = weight_x[x : x + 1] * weight_y
            weight_xy = hat_xy[n]
            pushed = jnp.concatenate([weight_xy * cell[d : d + 1] for d in range(3)], axis=0)
            push_high, push_low = halves(pushed)
            both = dot_nt(push_high, hat_z[n])
            part = both[:, 0:NZ] + both[:, NZ : 2 * NZ] + dot_nt(push_low, z_high)
            total = part if total is None else total + part
    force_send[...] = total.reshape(3, CX, CY, NZ)
    force_copy = to_pair(force_send, force_recv, 1)
    force_copy.start()

    z_rows = lax.broadcasted_iota(jnp.int32, (NZ, EDGE), 0)
    put_z = jnp.where(z_rows == (write_sites & (NZ - 1)), 1.0, 0.0).astype(jnp.bfloat16)
    xy_rows = lax.broadcasted_iota(jnp.int32, (XY, EDGE), 0)
    put_xy = jnp.where(xy_rows == (write_sites >> 7), 1.0, 0.0)
    written = dot_nt(put_xy.astype(jnp.bfloat16), put_z).reshape(CX, CY, NZ) > 0.5
    edge_copy.wait_recv()
    for i in range(19):
        row = edge_recv[i : i + 1, :]
        row_high = f32(row.astype(jnp.bfloat16))
        edge_high[i * XY : (i + 1) * XY] = (put_xy * row_high).astype(jnp.bfloat16)
        edge_low[i * XY : (i + 1) * XY] = (put_xy * (row - row_high)).astype(jnp.bfloat16)
    placed = dot_nt(edge_high[...], put_z) + dot_nt(edge_low[...], put_z)
    for i in range(19):
        new = placed[i * XY : (i + 1) * XY].reshape(CX, CY, NZ)
        lat[i] = jnp.where(written, new, lat[i])

    loads[5].wait()
    wet[...] = jnp.where(fluid[...] > 0, 1.0, 0.0)

    force_copy.wait_recv()
    for d in range(3):
        force[d] = force_send[d] + force_recv[d]
    relax = jnp.where(window, tau_fine, tau_coarse)
    inverse = jnp.where(window, 1.0 / tau_fine, 1.0 / tau_coarse)

    y_index = lax.broadcasted_iota(jnp.int32, (CX, CY, NZ), 1)
    z_index = lax.broadcasted_iota(jnp.int32, (CX, CY, NZ), 2)
    x_row = lax.broadcasted_iota(jnp.int32, (CX, NZ), 0)

    def shifted(block, move, low_x, high_x, low_y, high_y, corner):
        a, b, e = move
        if a == 1:
            block = jnp.concatenate([low_x[None], block[:-1]], axis=0)
        elif a == -1:
            block = jnp.concatenate([block[1:], high_x[None]], axis=0)
        if b != 0:
            side = low_y if b == 1 else high_y
            if a == 1:
                side = jnp.where(x_row == 0, corner, pltpu.roll(side, 1, 0))
            elif a == -1:
                side = jnp.where(x_row == CX - 1, corner, pltpu.roll(side, CX - 1, 0))
            block = pltpu.roll(block, 1 if b == 1 else CY - 1, 1)
            side = jnp.broadcast_to(side[:, None, :], (CX, CY, NZ))
            block = jnp.where(y_index == (0 if b == 1 else CY - 1), side, block)
        if e != 0:
            block = pltpu.roll(block, 1 if e == 1 else NZ - 1, 2)
        return block

    def sweep(turn):
        popul = [lat[i] for i in range(19)]
        density, momenta = moments(popul)
        velocity = [(momenta[d] + relax * force[d]) / density for d in range(3)]
        target = equilibrium(density, velocity)
        wet_here = wet[...] > 0.5
        for i in range(19):
            post[i] = jnp.where(wet_here, popul[i] - (popul[i] - target[i]) * inverse, popul[i])
        for k in range(5):
            face_send[turn, 0, k] = post[X_UP[k], CX - 1]
            face_send[turn, 1, k] = post[X_DOWN[k], 0]
            face_send[turn, 2, k] = post[Y_UP[k], :, CY - 1, :]
            face_send[turn, 3, k] = post[Y_DOWN[k], :, 0, :]
        face_send[turn, 0, 5] = wet[CX - 1]
        face_send[turn, 1, 5] = wet[0]
        face_send[turn, 2, 5] = wet[:, CY - 1, :]
        face_send[turn, 3, 5] = wet[:, 0, :]
        for k, i in enumerate(DIAGONAL):
            x = CX - 1 if lattice_c[i][0] == 1 else 0
            y = CY - 1 if lattice_c[i][1] == 1 else 0
            row_send[turn, k, 0:1] = post[i, x, y : y + 1, :]
            row_send[turn, k, 1:2] = wet[x, y : y + 1, :]
        copies = []
        places = [(g, up_s, t), (g, down_s, t), (g, s, up_t), (g, s, down_t)]
        for k in range(4):
            copies.append(
                pltpu.make_async_remote_copy(
                    src_ref=face_send.at[turn, k],
                    dst_ref=face_recv.at[turn, k],
                    send_sem=face_sems.at[turn, 0, k],
                    recv_sem=face_sems.at[turn, 1, k],
                    device_id=places[k],
                    device_id_type=MESH,
                )
            )
        for k, i in enumerate(DIAGONAL):
            copies.append(
                pltpu.make_async_remote_copy(
                    src_ref=row_send.at[turn, k],
                    dst_ref=row_recv.at[turn, k],
                    send_sem=row_sems.at[turn, 0, k],
                    recv_sem=row_sems.at[turn, 1, k],
                    device_id=(
                        g,
                        up_s if lattice_c[i][0] == 1 else down_s,
                        up_t if lattice_c[i][1] == 1 else down_t,
                    ),
                    device_id_type=MESH,
                )
            )
        for copy in copies:
            copy.start()
        for copy in copies:
            copy.wait_recv()
        if turn == 0:
            first_s = jnp.where(s > 0, 1.0, 0.0)
            last_s = jnp.where(s < slabs - 1, 1.0, 0.0)
            first_t = jnp.where(t > 0, 1.0, 0.0)
            last_t = jnp.where(t < TILES - 1, 1.0, 0.0)
            for i in range(1, 19):
                a, b, e = lattice_c[i]
                corner = None
                if i in DIAGONAL:
                    corner = row_recv[0, DIAGONAL.index(i), 1:2] * (
                        (first_s if a == 1 else last_s) * (first_t if b == 1 else last_t)
                    )
                moved = shifted(
                    wet[...],
                    lattice_c[i],
                    face_recv[0, 0, 5] * first_s,
                    face_recv[0, 1, 5] * last_s,
                    face_recv[0, 2, 5] * first_t,
                    face_recv[0, 3, 5] * last_t,
                    corner,
                )
                if e != 0:
                    moved = jnp.where(z_index == (0 if e == 1 else NZ - 1), 0.0, moved)
                open_mask[i] = moved
        for i in range(19):
            if i == 0:
                lat[0] = post[0]
                continue
            a, b, e = lattice_c[i]
            moved = shifted(
                post[i],
                lattice_c[i],
                face_recv[turn, 0, X_UP.index(i)] if a == 1 else None,
                face_recv[turn, 1, X_DOWN.index(i)] if a == -1 else None,
                face_recv[turn, 2, Y_UP.index(i)] if b == 1 else None,
                face_recv[turn, 3, Y_DOWN.index(i)] if b == -1 else None,
                row_recv[turn, DIAGONAL.index(i), 0:1] if i in DIAGONAL else None,
            )
            moved = jnp.where(open_mask[i] > 0.5, moved, post[opposite[i]])
            lat[i] = jnp.where(wet_here, moved, post[i])
        for copy in copies:
            copy.wait_send()

    sweep(0)

    @pl.when(window)
    def _():
        sweep(1)

    store_pop = pltpu.make_async_copy(lat, out_pop.at[0], out_sem.at[0])
    store_pop.start()

    density, momenta = moments([lat[i] for i in range(19)])
    for d in range(3):
        vel_send[d] = 0.5 * ((momenta[d] + 0.5 * force[d]) / density)
    vel_copy = to_pair(vel_send, vel_recv, 2)
    vel_copy.start()
    vel_copy.wait_recv()
    speed = (vel_send[...] + vel_recv[...]).reshape(3 * XY, NZ)
    speed_high, speed_low = halves(speed)
    speed_twice = jnp.concatenate([speed_high, speed_high], axis=1)

    ret_copies = [None] * TILES
    for j in (2, 1, 3, 0):
        for k in range(CAP):
            n = j * CAP + k
            seen = dot_nn(speed_twice, hat_z[n]) + dot_nn(speed_low, hat_z[n, 0:NZ])
            for d in range(3):
                reading = jnp.sum(seen[d * XY : (d + 1) * XY] * hat_xy[n], axis=0, keepdims=True)
                if j > 0:
                    ret_send[j, 3 * k + d : 3 * k + d + 1] = reading
                else:
                    ret_recv[j, 3 * k + d : 3 * k + d + 1] = reading
        if j > 0:
            ret_copies[j] = pltpu.make_async_remote_copy(
                src_ref=ret_send.at[j],
                dst_ref=ret_recv.at[j],
                send_sem=ret_sems.at[0, j],
                recv_sem=ret_sems.at[1, j],
                device_id=(g, s, tile_at[(TILES - j) % TILES]),
                device_id_type=MESH,
            )
            ret_copies[j].start()
    for j in range(1, TILES):
        ret_copies[j].wait_recv()
    for c in range(CELLS):
        value = None
        for j in range(TILES):
            for k in range(CAP):
                term = chosen(j, k, c) * ret_recv[j, 3 * k : 3 * k + 3]
                value = term if value is None else value + term
        for d in range(3):
            mine[d, c : c + 1] = value[d : d + 1, 0:VERTS]
    store_vel = pltpu.make_async_copy(mine, out_vel, out_sem.at[1])
    store_vel.start()

    for j in range(1, TILES):
        cell_copies[j].wait_send()
        ret_copies[j].wait_send()
    edge_copy.wait_send()
    force_copy.wait_send()
    vel_copy.wait_send()
    store_pop.wait()
    store_vel.wait()


def local(populations, fluid, couple, owner, vertex_site, frac, ref_shape):
    hbm = pl.BlockSpec(memory_space=pl.ANY)
    real = jnp.float32
    half = jnp.bfloat16
    new, velocity = pl.pallas_call(
        kernel,
        out_shape=(
            jax.ShapeDtypeStruct(populations.shape, real),
            jax.ShapeDtypeStruct((3, CELLS, VERTS), real),
        ),
        in_specs=[hbm, hbm, hbm, pl.BlockSpec(memory_space=pltpu.SMEM), hbm, hbm, hbm],
        out_specs=(hbm, hbm),
        scratch_shapes=[
            pltpu.VMEM((19, CX, CY, NZ), real),
            pltpu.VMEM((CX, CY, NZ), jnp.int32),
            pltpu.VMEM((2, 1, EDGE), jnp.int32),
            pltpu.VMEM((CELLS, VERTS), jnp.int32),
            pltpu.VMEM((3, CELLS, VERTS), real),
            pltpu.VMEM((3, CELLS, VERTS), real),
            pltpu.VMEM((CELLS, 8, PAD), real),
            pltpu.VMEM((TILES, CAP, 8, PAD), real),
            pltpu.VMEM((TILES, CAP, 8, PAD), real),
            pltpu.VMEM((19 * XY, 2 * NZ), half),
            pltpu.VMEM((19, EDGE), real),
            pltpu.VMEM((19, EDGE), real),
            pltpu.VMEM((19 * XY, EDGE), half),
            pltpu.VMEM((19 * XY, EDGE), half),
            pltpu.VMEM((TILES * CAP, XY, PAD), real),
            pltpu.VMEM((TILES * CAP, 2 * NZ, PAD), half),
            pltpu.VMEM((3, CX, CY, NZ), real),
            pltpu.VMEM((3, CX, CY, NZ), real),
            pltpu.VMEM((3, CX, CY, NZ), real),
            pltpu.VMEM((19, CX, CY, NZ), real),
            pltpu.VMEM((CX, CY, NZ), real),
            pltpu.VMEM((19, CX, CY, NZ), real),
            pltpu.VMEM((2, 4, 6, 8, NZ), real),
            pltpu.VMEM((2, 4, 6, 8, NZ), real),
            pltpu.VMEM((2, 4, 2, NZ), real),
            pltpu.VMEM((2, 4, 2, NZ), real),
            pltpu.VMEM((3, CX, CY, NZ), real),
            pltpu.VMEM((3, CX, CY, NZ), real),
            pltpu.VMEM((TILES, 6, PAD), real),
            pltpu.VMEM((TILES, 6, PAD), real),
            pltpu.VMEM((3, CELLS, VERTS), real),
            pltpu.SemaphoreType.DMA((6,)),
            pltpu.SemaphoreType.DMA((2,)),
            pltpu.SemaphoreType.DMA((2, TILES)),
            pltpu.SemaphoreType.DMA((2, 3)),
            pltpu.SemaphoreType.DMA((2, 2, 4)),
            pltpu.SemaphoreType.DMA((2, 2, 4)),
            pltpu.SemaphoreType.DMA((2, TILES)),
        ],
        compiler_params=pltpu.CompilerParams(
            collective_id=0, has_side_effects=True, vmem_limit_bytes=48 * 2**20
        ),
    )(
        populations,
        fluid,
        couple.reshape(2, 1, EDGE),
        owner.reshape(CELLS),
        vertex_site,
        jnp.transpose(frac, (1, 0, 2)),
        jnp.transpose(ref_shape, (1, 0, 2)),
    )
    return new, jnp.transpose(velocity, (1, 0, 2))


def solution(mesh):
    return jax.shard_map(
        local,
        mesh=mesh,
        in_specs=(
            P("group", None, "slab", "tile", None),
            P("group", "slab", "tile", None),
            P("group", "slab", "tile", None),
            P(("group", "slab", "tile"), None),
            P(("group", "slab", "tile"), None),
            P(("group", "slab", "tile"), None, None),
            P(("group", "slab", "tile"), None, None),
        ),
        out_specs=(
            P("group", None, "slab", "tile", None),
            P(("group", "slab", "tile"), None, None),
        ),
        check_vma=False,
    )
```

```python
import jax
import jax.numpy as jnp
from jax import lax
from jax.experimental import pallas as pl
from jax.experimental.pallas import tpu as pltpu
from jax.sharding import PartitionSpec as P

MESH = pl.DeviceIdType.MESH
CX = 8
CY = 8
NZ = 128
XY = CX * CY
VERTS = 642
PAD = 768
WIDE = 2 * PAD
CELLS = 4
CAP = 2
EDGE = 1024
TILES = 4

lattice_c = [
    (0, 0, 0),
    (1, 0, 0),
    (-1, 0, 0),
    (0, 1, 0),
    (0, -1, 0),
    (0, 0, 1),
    (0, 0, -1),
    (1, 1, 0),
    (-1, -1, 0),
    (1, -1, 0),
    (-1, 1, 0),
    (1, 0, 1),
    (-1, 0, -1),
    (1, 0, -1),
    (-1, 0, 1),
    (0, 1, 1),
    (0, -1, -1),
    (0, 1, -1),
    (0, -1, 1),
]
lattice_w = [1.0 / 3.0] + [1.0 / 18.0] * 6 + [1.0 / 36.0] * 12
opposite = [0, 2, 1, 4, 3, 6, 5, 8, 7, 10, 9, 12, 11, 14, 13, 16, 15, 18, 17]
tau_coarse = 0.8
tau_fine = 1.1
stiffness = 0.01

X_UP = [i for i in range(19) if lattice_c[i][0] == 1]
X_DOWN = [i for i in range(19) if lattice_c[i][0] == -1]
Y_UP = [i for i in range(19) if lattice_c[i][1] == 1]
Y_DOWN = [i for i in range(19) if lattice_c[i][1] == -1]
DIAGONAL = [7, 8, 9, 10]


def f32(x):
    return x.astype(jnp.float32)


def halves(x):
    high = x.astype(jnp.bfloat16)
    low = (x - f32(high)).astype(jnp.bfloat16)
    return high, low


def dot_nn(a, b):
    return lax.dot_general(a, b, (((1,), (0,)), ((), ())), preferred_element_type=jnp.float32)


def dot_nt(a, b):
    return lax.dot_general(a, b, (((1,), (1,)), ((), ())), preferred_element_type=jnp.float32)


def moments(popul):
    density = popul[0]
    momenta = [None, None, None]
    for i in range(1, 19):
        density = density + popul[i]
        for d in range(3):
            sign = lattice_c[i][d]
            if sign == 0:
                continue
            if momenta[d] is None:
                momenta[d] = popul[i]
            elif sign > 0:
                momenta[d] = momenta[d] + popul[i]
            else:
                momenta[d] = momenta[d] - popul[i]
    return density, momenta


def equilibrium(density, velocity):
    ux, uy, uz = velocity
    base = 1.0 - 1.5 * (ux * ux + uy * uy + uz * uz)
    terms = [None] * 19
    terms[0] = lattice_w[0] * density * base
    for i in range(1, 19, 2):
        along = None
        for d in range(3):
            sign = lattice_c[i][d]
            if sign == 0:
                continue
            if along is None:
                along = velocity[d]
            elif sign > 0:
                along = along + velocity[d]
            else:
                along = along - velocity[d]
        weight = lattice_w[i] * density
        even = base + 4.5 * along * along
        odd = 3.0 * along
        terms[i] = weight * (even + odd)
        terms[i + 1] = weight * (even - odd)
    return terms


def kernel(
    pop_hbm,
    fluid_hbm,
    couple_hbm,
    owner_ref,
    site_hbm,
    frac_hbm,
    shape_hbm,
    out_pop,
    out_vel,
    fluid,
    couple,
    site,
    frac,
    rest,
    payload,
    cell_send,
    cell_recv,
    pop_half,
    edge_send,
    edge_recv,
    edge_high,
    edge_low,
    hat_xy,
    hat_z,
    force,
    post,
    wet,
    open_mask,
    face_send,
    face_recv,
    row_send,
    row_recv,
    vel_send,
    vel_recv,
    ret_send,
    ret_recv,
    in_sem,
    cell_sems,
    pair_sems,
    face_sems,
    row_sems,
    ret_send_sems,
    ret_recv_sems,
):
    lat = out_pop.at[0]
    g = lax.axis_index("group")
    s = lax.axis_index("slab")
    t = lax.axis_index("tile")
    slabs = lax.axis_size("slab")
    window = g == 1
    up_s, down_s = lax.rem(s + 1, slabs), lax.rem(s + slabs - 1, slabs)
    tile_at = [lax.rem(t + j, TILES) for j in range(TILES)]
    other = 1 - g
    has_x = {1: s < slabs - 1, -1: s > 0, 0: True}
    has_y = {1: t < TILES - 1, -1: t > 0, 0: True}
    at_x = {1: up_s, -1: down_s, 0: s}
    at_y = {1: tile_at[1], -1: tile_at[3], 0: t}

    def exists(a, b):
        if a == 0:
            return has_y[b]
        if b == 0:
            return has_x[a]
        return has_x[a] & has_y[b]

    loads = [
        pltpu.make_async_copy(src, dst, in_sem.at[k])
        for k, (src, dst) in enumerate(
            [
                (site_hbm, site),
                (frac_hbm, frac),
                (shape_hbm, rest),
                (couple_hbm, couple),
                (pop_hbm.at[0], lat),
                (fluid_hbm.at[0], fluid),
            ]
        )
    ]
    for load in loads:
        load.start()

    barrier = pltpu.get_barrier_semaphore()
    expected = 2 * TILES - 1
    for dg in range(2):
        for j in range(TILES):
            if dg + j > 0:
                pl.semaphore_signal(
                    barrier,
                    inc=1,
                    device_id=(other if dg else g, s, tile_at[j]),
                    device_id_type=MESH,
                )
    for a, b in ((1, 0), (-1, 0), (1, 1), (1, -1), (-1, 1), (-1, -1)):
        there = exists(a, b)
        expected = expected + jnp.where(there, 1, 0)

        @pl.when(there)
        def _():
            pl.semaphore_signal(
                barrier, inc=1, device_id=(g, at_x[a], at_y[b]), device_id_type=MESH
            )

    payload[...] = jnp.zeros_like(payload)
    for load in loads[:3]:
        load.wait()
    site_value = site[...]
    coords = [
        site_value >> 10,
        (site_value >> 7) & (CY - 1),
        site_value & (NZ - 1),
    ]
    for d in range(3):
        offset = frac[d]
        position = f32(coords[d]) + offset
        centre = jnp.sum(position, axis=1, keepdims=True) * (1.0 / VERTS)
        push = -stiffness * (position - centre - rest[d])
        for c in range(CELLS):
            payload[c, d : d + 1, 0:VERTS] = push[c : c + 1]
            payload[c, 3 + d : 4 + d, 0:VERTS] = offset[c : c + 1]
    for c in range(CELLS):
        payload[c, 6:7, 0:VERTS] = f32(site_value[c : c + 1])

    owners = [owner_ref[c] for c in range(CELLS)]
    ranks = []
    for c in range(CELLS):
        rank = jnp.int32(0)
        for before in range(c):
            rank = rank + jnp.where(owners[before] == owners[c], 1, 0)
        ranks.append(rank)

    def chosen(j, k, c):
        return jnp.where((owners[c] == tile_at[j]) & (ranks[c] == k), 1.0, 0.0)

    for j in range(TILES):
        for k in range(CAP):
            slot = chosen(j, k, 0) * payload[0]
            for c in range(1, CELLS):
                slot = slot + chosen(j, k, c) * payload[c]
            cell_send[j, :, k * PAD : (k + 1) * PAD] = slot
            if j == 0:
                cell_recv[0, 0, :, k * PAD : (k + 1) * PAD] = slot

    pl.semaphore_wait(barrier, expected)

    cell_copies = {}
    for dg, j in ((1, 2), (0, 2), (1, 1), (1, 3), (1, 0), (0, 1), (0, 3)):
        copy = pltpu.make_async_remote_copy(
            src_ref=cell_send.at[j],
            dst_ref=cell_recv.at[dg, j],
            send_sem=cell_sems.at[0, dg, j],
            recv_sem=cell_sems.at[1, dg, j],
            device_id=(other if dg else g, s, tile_at[j]),
            device_id_type=MESH,
        )
        copy.start()
        cell_copies[dg, j] = copy

    def to_pair(src, dst, k):
        return pltpu.make_async_remote_copy(
            src_ref=src,
            dst_ref=dst,
            send_sem=pair_sems.at[0, k],
            recv_sem=pair_sems.at[1, k],
            device_id=(other, s, t),
            device_id_type=MESH,
        )

    loads[3].wait()
    loads[4].wait()
    row_0, row_1 = couple[0], couple[1]
    read_sites = row_0 + g * (row_1 - row_0)
    write_sites = row_1 + g * (row_0 - row_1)
    high, low = halves(lat[...].reshape(19 * XY, NZ))
    pop_half[:, 0:NZ] = high
    pop_half[:, NZ : 2 * NZ] = low
    chunk = 256
    for k in range(EDGE // chunk):
        sites = read_sites[:, k * chunk : (k + 1) * chunk]
        z_rows = lax.broadcasted_iota(jnp.int32, (NZ, chunk), 0)
        pick_z = jnp.where(z_rows == (sites & (NZ - 1)), 1.0, 0.0).astype(jnp.bfloat16)
        pick_z = jnp.concatenate([pick_z, pick_z], axis=0)
        xy_rows = lax.broadcasted_iota(jnp.int32, (XY, chunk), 0)
        pick_xy = jnp.where(xy_rows == (sites >> 7), 1.0, 0.0)
        found = dot_nn(pop_half[...], pick_z)
        for i in range(19):
            edge_send[i : i + 1, k * chunk : (k + 1) * chunk] = jnp.sum(
                found[i * XY : (i + 1) * XY] * pick_xy, axis=0, keepdims=True
            )
    rows = [edge_send[i : i + 1, :] for i in range(19)]
    density, momenta = moments(rows)
    target = equilibrium(density, [m / density for m in momenta])
    factor = jnp.where(window, 2.0 * tau_coarse / tau_fine, tau_fine / (2.0 * tau_coarse))
    for i in range(19):
        edge_send[i : i + 1, :] = target[i] + factor * (rows[i] - target[i])
    edge_copy = to_pair(edge_send, edge_recv, 0)
    edge_copy.start()

    def spread(dg, j):
        cell = cell_recv[dg, j]
        where_at = cell[6:7].astype(jnp.int32)
        z_rows = lax.broadcasted_iota(jnp.int32, (NZ, WIDE), 0) - (where_at & (NZ - 1))
        frac_z = cell[5:6]
        weight_z = jnp.where(z_rows == 0, 1.0 - frac_z, jnp.where(z_rows == 1, frac_z, 0.0))
        z_high, z_low = halves(weight_z)
        hat_z[dg, j, 0:NZ] = z_high
        hat_z[dg, j, NZ : 2 * NZ] = z_low
        y_rows = lax.broadcasted_iota(jnp.int32, (CY, WIDE), 0) - ((where_at >> 7) & (CY - 1))
        frac_y = cell[4:5]
        weight_y = jnp.where(y_rows == 0, 1.0 - frac_y, jnp.where(y_rows == 1, frac_y, 0.0))
        x_rows = lax.broadcasted_iota(jnp.int32, (CX, WIDE), 0) - (where_at >> 10)
        frac_x = cell[3:4]
        weight_x = jnp.where(x_rows == 0, 1.0 - frac_x, jnp.where(x_rows == 1, frac_x, 0.0))
        for x in range(CX):
            hat_xy[dg, j, x * CY : (x + 1) * CY] = weight_x[x : x + 1] * weight_y
        weight_xy = hat_xy[dg, j]
        pushed = jnp.concatenate([weight_xy * cell[d : d + 1] for d in range(3)], axis=0)
        push_high, push_low = halves(pushed)
        both = dot_nt(jnp.concatenate([push_high, push_low], axis=0), hat_z[dg, j])
        high_rows, low_rows = both[0 : 3 * XY], both[3 * XY :]
        return high_rows[:, 0:NZ] + high_rows[:, NZ : 2 * NZ] + low_rows[:, 0:NZ]

    total = spread(0, 0)
    for dg, j in ((0, 1), (0, 3), (1, 0)):
        cell_copies[dg, j].wait_recv()
        total = total + spread(dg, j)

    z_rows = lax.broadcasted_iota(jnp.int32, (NZ, EDGE), 0)
    put_z = jnp.where(z_rows == (write_sites & (NZ - 1)), 1.0, 0.0).astype(jnp.bfloat16)
    xy_rows = lax.broadcasted_iota(jnp.int32, (XY, EDGE), 0)
    put_xy = jnp.where(xy_rows == (write_sites >> 7), 1.0, 0.0)
    written = dot_nt(put_xy.astype(jnp.bfloat16), put_z).reshape(CX, CY, NZ) > 0.5
    edge_copy.wait_recv()
    for i in range(19):
        row = edge_recv[i : i + 1, :]
        row_high = f32(row.astype(jnp.bfloat16))
        edge_high[i * XY : (i + 1) * XY] = (put_xy * row_high).astype(jnp.bfloat16)
        edge_low[i * XY : (i + 1) * XY] = (put_xy * (row - row_high)).astype(jnp.bfloat16)
    placed = dot_nt(edge_high[...], put_z) + dot_nt(edge_low[...], put_z)
    for i in range(19):
        new = placed[i * XY : (i + 1) * XY].reshape(CX, CY, NZ)
        lat[i] = jnp.where(written, new, lat[i])

    for dg, j in ((1, 1), (1, 3), (0, 2), (1, 2)):
        cell_copies[dg, j].wait_recv()
        total = total + spread(dg, j)
    for d in range(3):
        force[d] = total[d * XY : (d + 1) * XY].reshape(CX, CY, NZ)

    loads[5].wait()
    wet[...] = jnp.where(fluid[...] > 0, 1.0, 0.0)

    relax = jnp.where(window, tau_fine, tau_coarse)
    inverse = jnp.where(window, 1.0 / tau_fine, 1.0 / tau_coarse)

    y_index = lax.broadcasted_iota(jnp.int32, (CX, CY, NZ), 1)
    z_index = lax.broadcasted_iota(jnp.int32, (CX, CY, NZ), 2)
    x_row = lax.broadcasted_iota(jnp.int32, (CX, NZ), 0)

    def shifted(block, move, low_x, high_x, low_y, high_y, corner):
        a, b, e = move
        if a == 1:
            block = jnp.concatenate([low_x[None], block[:-1]], axis=0)
        elif a == -1:
            block = jnp.concatenate([block[1:], high_x[None]], axis=0)
        if b != 0:
            side = low_y if b == 1 else high_y
            if a == 1:
                side = jnp.where(x_row == 0, corner, pltpu.roll(side, 1, 0))
            elif a == -1:
                side = jnp.where(x_row == CX - 1, corner, pltpu.roll(side, CX - 1, 0))
            block = pltpu.roll(block, 1 if b == 1 else CY - 1, 1)
            side = jnp.broadcast_to(side[:, None, :], (CX, CY, NZ))
            block = jnp.where(y_index == (0 if b == 1 else CY - 1), side, block)
        if e != 0:
            block = pltpu.roll(block, 1 if e == 1 else NZ - 1, 2)
        return block

    def sweep(turn):
        popul = [lat[i] for i in range(19)]
        density, momenta = moments(popul)
        velocity = [(momenta[d] + relax * force[d]) / density for d in range(3)]
        target = equilibrium(density, velocity)
        wet_here = wet[...] > 0.5
        for i in range(19):
            post[i] = jnp.where(wet_here, popul[i] - (popul[i] - target[i]) * inverse, popul[i])
        for k in range(5):
            face_send[turn, 0, k] = post[X_UP[k], CX - 1]
            face_send[turn, 1, k] = post[X_DOWN[k], 0]
            face_send[turn, 2, k] = post[Y_UP[k], :, CY - 1, :]
            face_send[turn, 3, k] = post[Y_DOWN[k], :, 0, :]
        face_send[turn, 0, 5] = wet[CX - 1]
        face_send[turn, 1, 5] = wet[0]
        face_send[turn, 2, 5] = wet[:, CY - 1, :]
        face_send[turn, 3, 5] = wet[:, 0, :]
        for k, i in enumerate(DIAGONAL):
            x = CX - 1 if lattice_c[i][0] == 1 else 0
            y = CY - 1 if lattice_c[i][1] == 1 else 0
            row_send[turn, k, 0:1] = post[i, x, y : y + 1, :]
            row_send[turn, k, 1:2] = wet[x, y : y + 1, :]
        copies = []
        moves = [(1, 0), (-1, 0), (0, 1), (0, -1)]
        for k in range(4):
            copies.append(
                (
                    moves[k],
                    pltpu.make_async_remote_copy(
                        src_ref=face_send.at[turn, k],
                        dst_ref=face_recv.at[turn, k],
                        send_sem=face_sems.at[turn, 0, k],
                        recv_sem=face_sems.at[turn, 1, k],
                        device_id=(g, at_x[moves[k][0]], at_y[moves[k][1]]),
                        device_id_type=MESH,
                    ),
                )
            )
        for k, i in enumerate(DIAGONAL):
            a, b, _ = lattice_c[i]
            copies.append(
                (
                    (a, b),
                    pltpu.make_async_remote_copy(
                        src_ref=row_send.at[turn, k],
                        dst_ref=row_recv.at[turn, k],
                        send_sem=row_sems.at[turn, 0, k],
                        recv_sem=row_sems.at[turn, 1, k],
                        device_id=(g, at_x[a], at_y[b]),
                        device_id_type=MESH,
                    ),
                )
            )
        for (a, b), copy in reversed(copies):
            pl.when(exists(a, b))(copy.start)
        for (a, b), copy in copies:
            pl.when(exists(-a, -b))(copy.wait_recv)
        if turn == 0:
            ones = jnp.ones((8, NZ), jnp.int32)

            def known(flags, a, b):
                if a != 0:
                    flags = jnp.where(ones * s != (0 if a == 1 else slabs - 1), flags, 0.0)
                if b != 0:
                    flags = jnp.where(ones * t != (0 if b == 1 else TILES - 1), flags, 0.0)
                return flags

            for i in range(1, 19):
                a, b, e = lattice_c[i]
                corner = None
                if i in DIAGONAL:
                    k = DIAGONAL.index(i)
                    corner = known(jnp.broadcast_to(row_recv[0, k, 1:2], (8, NZ)), a, b)
                moved = shifted(
                    wet[...],
                    lattice_c[i],
                    known(face_recv[0, 0, 5], 1, 0),
                    known(face_recv[0, 1, 5], -1, 0),
                    known(face_recv[0, 2, 5], 0, 1),
                    known(face_recv[0, 3, 5], 0, -1),
                    corner,
                )
                if e != 0:
                    moved = jnp.where(z_index == (0 if e == 1 else NZ - 1), 0.0, moved)
                open_mask[i] = moved
        for i in range(19):
            if i == 0:
                lat[0] = post[0]
                continue
            a, b, e = lattice_c[i]
            moved = shifted(
                post[i],
                lattice_c[i],
                face_recv[turn, 0, X_UP.index(i)] if a == 1 else None,
                face_recv[turn, 1, X_DOWN.index(i)] if a == -1 else None,
                face_recv[turn, 2, Y_UP.index(i)] if b == 1 else None,
                face_recv[turn, 3, Y_DOWN.index(i)] if b == -1 else None,
                row_recv[turn, DIAGONAL.index(i), 0:1] if i in DIAGONAL else None,
            )
            moved = jnp.where(open_mask[i] > 0.5, moved, post[opposite[i]])
            lat[i] = jnp.where(wet_here, moved, post[i])
        for (a, b), copy in copies:
            pl.when(exists(a, b))(copy.wait_send)

    def half_velocity():
        density, momenta = moments([lat[i] for i in range(19)])
        for d in range(3):
            vel_send[d] = 0.5 * ((momenta[d] + 0.5 * force[d]) / density)

    sweep(0)
    vel_copy = to_pair(vel_send, vel_recv, 1)

    def return_copy(dg, j):
        return pltpu.make_async_remote_copy(
            src_ref=ret_send.at[dg, j],
            dst_ref=ret_recv.at[j],
            send_sem=ret_send_sems.at[dg, j],
            recv_sem=ret_recv_sems.at[j],
            device_id=(other if dg else g, s, tile_at[(TILES - j) % TILES]),
            device_id_type=MESH,
        )

    @pl.when(g == 0)
    def _():
        half_velocity()
        vel_copy.start()
        return_copy(1, 0).wait_recv()
        vel_copy.wait_send()

    @pl.when(window)
    def _():
        sweep(1)
        half_velocity()
        vel_copy.wait_recv()
        speed = (vel_send[...] + vel_recv[...]).reshape(3 * XY, NZ)
        speed_high, speed_low = halves(speed)
        speed_twice = jnp.concatenate([speed_high, speed_high], axis=1)
        for dg, j in ((1, 2), (1, 1), (1, 3), (1, 0), (0, 2), (0, 1), (0, 3), (0, 0)):
            seen = dot_nn(speed_twice, hat_z[dg, j]) + dot_nn(speed_low, hat_z[dg, j, 0:NZ])
            for d in range(3):
                reading = jnp.sum(
                    seen[d * XY : (d + 1) * XY] * hat_xy[dg, j], axis=0, keepdims=True
                )
                if dg + j > 0:
                    ret_send[dg, j, d : d + 1] = reading
                else:
                    ret_recv[0, d : d + 1] = reading
            if dg + j > 0:
                return_copy(dg, j).start()
        for dg in range(2):
            for j in range(TILES):
                if dg + j > 0:
                    return_copy(dg, j).wait_send()

    for j in range(1, TILES):
        return_copy(0, j).wait_recv()
    for c in range(CELLS):
        value = None
        for j in range(TILES):
            for k in range(CAP):
                term = chosen(j, k, c) * ret_recv[j, :, k * PAD : (k + 1) * PAD]
                value = term if value is None else value + term
        for d in range(3):
            out_vel[d, c : c + 1] = value[d : d + 1, 0:VERTS]

    for copy in cell_copies.values():
        copy.wait_send()
    edge_copy.wait_send()


def local(populations, fluid, couple, owner, vertex_site, frac, ref_shape):
    hbm = pl.BlockSpec(memory_space=pl.ANY)
    vmem = pl.BlockSpec(memory_space=pltpu.VMEM)
    real = jnp.float32
    half = jnp.bfloat16
    new, velocity = pl.pallas_call(
        kernel,
        out_shape=(
            pltpu.VMEM(populations.shape, real),
            pltpu.VMEM((3, CELLS, VERTS), real),
        ),
        in_specs=[hbm, hbm, hbm, pl.BlockSpec(memory_space=pltpu.SMEM), hbm, hbm, hbm],
        out_specs=(vmem, vmem),
        scratch_shapes=[
            pltpu.VMEM((CX, CY, NZ), jnp.int32),
            pltpu.VMEM((2, 1, EDGE), jnp.int32),
            pltpu.VMEM((CELLS, VERTS), jnp.int32),
            pltpu.VMEM((3, CELLS, VERTS), real),
            pltpu.VMEM((3, CELLS, VERTS), real),
            pltpu.VMEM((CELLS, 8, PAD), real),
            pltpu.VMEM((TILES, 8, WIDE), real),
            pltpu.VMEM((2, TILES, 8, WIDE), real),
            pltpu.VMEM((19 * XY, 2 * NZ), half),
            pltpu.VMEM((19, EDGE), real),
            pltpu.VMEM((19, EDGE), real),
            pltpu.VMEM((19 * XY, EDGE), half),
            pltpu.VMEM((19 * XY, EDGE), half),
            pltpu.VMEM((2, TILES, XY, WIDE), real),
            pltpu.VMEM((2, TILES, 2 * NZ, WIDE), half),
            pltpu.VMEM((3, CX, CY, NZ), real),
            pltpu.VMEM((19, CX, CY, NZ), real),
            pltpu.VMEM((CX, CY, NZ), real),
            pltpu.VMEM((19, CX, CY, NZ), real),
            pltpu.VMEM((2, 4, 6, 8, NZ), real),
            pltpu.VMEM((2, 4, 6, 8, NZ), real),
            pltpu.VMEM((2, 4, 2, NZ), real),
            pltpu.VMEM((2, 4, 2, NZ), real),
            pltpu.VMEM((3, CX, CY, NZ), real),
            pltpu.VMEM((3, CX, CY, NZ), real),
            pltpu.VMEM((2, TILES, 3, WIDE), real),
            pltpu.VMEM((TILES, 3, WIDE), real),
            pltpu.SemaphoreType.DMA((6,)),
            pltpu.SemaphoreType.DMA((2, 2, TILES)),
            pltpu.SemaphoreType.DMA((2, 2)),
            pltpu.SemaphoreType.DMA((2, 2, 4)),
            pltpu.SemaphoreType.DMA((2, 2, 4)),
            pltpu.SemaphoreType.DMA((2, TILES)),
            pltpu.SemaphoreType.DMA((TILES,)),
        ],
        compiler_params=pltpu.CompilerParams(
            collective_id=0, has_side_effects=True, vmem_limit_bytes=62 * 2**20
        ),
    )(
        populations,
        fluid,
        couple.reshape(2, 1, EDGE),
        owner.reshape(CELLS),
        vertex_site,
        jnp.transpose(frac, (1, 0, 2)),
        jnp.transpose(ref_shape, (1, 0, 2)),
    )
    return new, jnp.transpose(velocity, (1, 0, 2))


def solution(mesh):
    return jax.shard_map(
        local,
        mesh=mesh,
        in_specs=(
            P("group", None, "slab", "tile", None),
            P("group", "slab", "tile", None),
            P("group", "slab", "tile", None),
            P(("group", "slab", "tile"), None),
            P(("group", "slab", "tile"), None),
            P(("group", "slab", "tile"), None, None),
            P(("group", "slab", "tile"), None, None),
        ),
        out_specs=(
            P("group", None, "slab", "tile", None),
            P(("group", "slab", "tile"), None, None),
        ),
        check_vma=False,
    )
```

```python
import jax
import jax.numpy as jnp
from jax import lax
from jax.experimental import pallas as pl
from jax.experimental.pallas import tpu as pltpu
from jax.sharding import PartitionSpec as P

MESH = pl.DeviceIdType.MESH
CX = 8
CY = 8
NZ = 128
XY = CX * CY
VERTS = 642
PAD = 768
WIDE = 2 * PAD
CELLS = 4
CAP = 2
EDGE = 1024
TILES = 4

lattice_c = [
    (0, 0, 0),
    (1, 0, 0),
    (-1, 0, 0),
    (0, 1, 0),
    (0, -1, 0),
    (0, 0, 1),
    (0, 0, -1),
    (1, 1, 0),
    (-1, -1, 0),
    (1, -1, 0),
    (-1, 1, 0),
    (1, 0, 1),
    (-1, 0, -1),
    (1, 0, -1),
    (-1, 0, 1),
    (0, 1, 1),
    (0, -1, -1),
    (0, 1, -1),
    (0, -1, 1),
]
lattice_w = [1.0 / 3.0] + [1.0 / 18.0] * 6 + [1.0 / 36.0] * 12
opposite = [0, 2, 1, 4, 3, 6, 5, 8, 7, 10, 9, 12, 11, 14, 13, 16, 15, 18, 17]
tau_coarse = 0.8
tau_fine = 1.1
stiffness = 0.01

X_UP = [i for i in range(19) if lattice_c[i][0] == 1]
X_DOWN = [i for i in range(19) if lattice_c[i][0] == -1]
Y_UP = [i for i in range(19) if lattice_c[i][1] == 1]
Y_DOWN = [i for i in range(19) if lattice_c[i][1] == -1]
DIAGONAL = [7, 8, 9, 10]


def f32(x):
    return x.astype(jnp.float32)


def halves(x):
    high = x.astype(jnp.bfloat16)
    low = (x - f32(high)).astype(jnp.bfloat16)
    return high, low


def dot_nn(a, b):
    return lax.dot_general(a, b, (((1,), (0,)), ((), ())), preferred_element_type=jnp.float32)


def dot_nt(a, b):
    return lax.dot_general(a, b, (((1,), (1,)), ((), ())), preferred_element_type=jnp.float32)


def moments(popul):
    density = popul[0]
    momenta = [None, None, None]
    for i in range(1, 19):
        density = density + popul[i]
        for d in range(3):
            sign = lattice_c[i][d]
            if sign == 0:
                continue
            if momenta[d] is None:
                momenta[d] = popul[i]
            elif sign > 0:
                momenta[d] = momenta[d] + popul[i]
            else:
                momenta[d] = momenta[d] - popul[i]
    return density, momenta


def equilibrium(density, velocity):
    ux, uy, uz = velocity
    base = 1.0 - 1.5 * (ux * ux + uy * uy + uz * uz)
    terms = [None] * 19
    terms[0] = lattice_w[0] * density * base
    for i in range(1, 19, 2):
        along = None
        for d in range(3):
            sign = lattice_c[i][d]
            if sign == 0:
                continue
            if along is None:
                along = velocity[d]
            elif sign > 0:
                along = along + velocity[d]
            else:
                along = along - velocity[d]
        weight = lattice_w[i] * density
        even = base + 4.5 * along * along
        odd = 3.0 * along
        terms[i] = weight * (even + odd)
        terms[i + 1] = weight * (even - odd)
    return terms


def kernel(
    pop_hbm,
    fluid_hbm,
    couple_hbm,
    owner_ref,
    site_hbm,
    frac_hbm,
    shape_hbm,
    out_pop,
    out_vel,
    fluid,
    couple,
    site,
    frac,
    rest,
    payload,
    cell_send,
    cell_recv,
    pop_half,
    edge_send,
    edge_recv,
    edge_high,
    edge_low,
    hat_xy,
    hat_z,
    force_send,
    force_recv,
    force,
    post,
    wet,
    open_mask,
    face_send,
    face_recv,
    row_send,
    row_recv,
    vel_send,
    vel_recv,
    ret_send,
    ret_recv,
    in_sem,
    cell_sems,
    pair_sems,
    face_sems,
    row_sems,
    ret_send_sems,
    ret_recv_sems,
):
    lat = out_pop.at[0]
    g = lax.axis_index("group")
    s = lax.axis_index("slab")
    t = lax.axis_index("tile")
    slabs = lax.axis_size("slab")
    window = g == 1
    up_s, down_s = lax.rem(s + 1, slabs), lax.rem(s + slabs - 1, slabs)
    tile_at = [lax.rem(t + j, TILES) for j in range(TILES)]
    other = 1 - g
    has_x = {1: s < slabs - 1, -1: s > 0, 0: True}
    has_y = {1: t < TILES - 1, -1: t > 0, 0: True}
    at_x = {1: up_s, -1: down_s, 0: s}
    at_y = {1: tile_at[1], -1: tile_at[3], 0: t}

    def exists(a, b):
        if a == 0:
            return has_y[b]
        if b == 0:
            return has_x[a]
        return has_x[a] & has_y[b]

    loads = [
        pltpu.make_async_copy(src, dst, in_sem.at[k])
        for k, (src, dst) in enumerate(
            [
                (site_hbm, site),
                (frac_hbm, frac),
                (shape_hbm, rest),
                (couple_hbm, couple),
                (pop_hbm.at[0], lat),
                (fluid_hbm.at[0], fluid),
            ]
        )
    ]
    for load in loads:
        load.start()

    barrier = pltpu.get_barrier_semaphore()
    expected = 2 * TILES - 1
    for dg in range(2):
        for j in range(TILES):
            if dg + j > 0:
                pl.semaphore_signal(
                    barrier,
                    inc=1,
                    device_id=(other if dg else g, s, tile_at[j]),
                    device_id_type=MESH,
                )
    for a, b in ((1, 0), (-1, 0), (1, 1), (1, -1), (-1, 1), (-1, -1)):
        there = exists(a, b)
        expected = expected + jnp.where(there, 1, 0)

        @pl.when(there)
        def _():
            pl.semaphore_signal(
                barrier, inc=1, device_id=(g, at_x[a], at_y[b]), device_id_type=MESH
            )

    payload[...] = jnp.zeros_like(payload)
    for load in loads[:3]:
        load.wait()
    site_value = site[...]
    coords = [
        site_value >> 10,
        (site_value >> 7) & (CY - 1),
        site_value & (NZ - 1),
    ]
    for d in range(3):
        offset = frac[d]
        position = f32(coords[d]) + offset
        centre = jnp.sum(position, axis=1, keepdims=True) * (1.0 / VERTS)
        push = -stiffness * (position - centre - rest[d])
        for c in range(CELLS):
            payload[c, d : d + 1, 0:VERTS] = offset[c : c + 1]
            payload[c, 4 + d : 5 + d, 0:VERTS] = push[c : c + 1]
    for c in range(CELLS):
        payload[c, 3:4, 0:VERTS] = f32(site_value[c : c + 1])

    owners = [owner_ref[c] for c in range(CELLS)]
    ranks = []
    for c in range(CELLS):
        rank = jnp.int32(0)
        for before in range(c):
            rank = rank + jnp.where(owners[before] == owners[c], 1, 0)
        ranks.append(rank)

    def chosen(j, k, c):
        return jnp.where((owners[c] == tile_at[j]) & (ranks[c] == k), 1.0, 0.0)

    for j in range(TILES):
        for k in range(CAP):
            slot = chosen(j, k, 0) * payload[0]
            for c in range(1, CELLS):
                slot = slot + chosen(j, k, c) * payload[c]
            cell_send[j, :, k * PAD : (k + 1) * PAD] = slot
            if j == 0:
                cell_recv[0, 0, :, k * PAD : (k + 1) * PAD] = slot

    def to_pair(src, dst, k):
        return pltpu.make_async_remote_copy(
            src_ref=src,
            dst_ref=dst,
            send_sem=pair_sems.at[0, k],
            recv_sem=pair_sems.at[1, k],
            device_id=(other, s, t),
            device_id_type=MESH,
        )

    loads[3].wait()
    loads[4].wait()
    row_0, row_1 = couple[0], couple[1]
    read_sites = row_0 + g * (row_1 - row_0)
    write_sites = row_1 + g * (row_0 - row_1)
    high, low = halves(lat[...].reshape(19 * XY, NZ))
    pop_half[:, 0:NZ] = high
    pop_half[:, NZ : 2 * NZ] = low
    chunk = 256
    for k in range(EDGE // chunk):
        sites = read_sites[:, k * chunk : (k + 1) * chunk]
        z_rows = lax.broadcasted_iota(jnp.int32, (NZ, chunk), 0)
        pick_z = jnp.where(z_rows == (sites & (NZ - 1)), 1.0, 0.0).astype(jnp.bfloat16)
        pick_z = jnp.concatenate([pick_z, pick_z], axis=0)
        xy_rows = lax.broadcasted_iota(jnp.int32, (XY, chunk), 0)
        pick_xy = jnp.where(xy_rows == (sites >> 7), 1.0, 0.0)
        found = dot_nn(pop_half[...], pick_z)
        for i in range(19):
            edge_send[i : i + 1, k * chunk : (k + 1) * chunk] = jnp.sum(
                found[i * XY : (i + 1) * XY] * pick_xy, axis=0, keepdims=True
            )
    rows = [edge_send[i : i + 1, :] for i in range(19)]
    density, momenta = moments(rows)
    target = equilibrium(density, [m / density for m in momenta])
    factor = jnp.where(window, 2.0 * tau_coarse / tau_fine, tau_fine / (2.0 * tau_coarse))
    for i in range(19):
        edge_send[i : i + 1, :] = target[i] + factor * (rows[i] - target[i])

    def hats(dg, j):
        cell = cell_recv[dg, j, 0:4]
        where_at = cell[3:4].astype(jnp.int32)
        z_rows = lax.broadcasted_iota(jnp.int32, (NZ, WIDE), 0) - (where_at & (NZ - 1))
        frac_z = cell[2:3]
        weight_z = jnp.where(z_rows == 0, 1.0 - frac_z, jnp.where(z_rows == 1, frac_z, 0.0))
        z_high, z_low = halves(weight_z)
        hat_z[dg, j, 0:NZ] = z_high
        hat_z[dg, j, NZ : 2 * NZ] = z_low
        y_rows = lax.broadcasted_iota(jnp.int32, (CY, WIDE), 0) - ((where_at >> 7) & (CY - 1))
        frac_y = cell[1:2]
        weight_y = jnp.where(y_rows == 0, 1.0 - frac_y, jnp.where(y_rows == 1, frac_y, 0.0))
        x_rows = lax.broadcasted_iota(jnp.int32, (CX, WIDE), 0) - (where_at >> 10)
        frac_x = cell[0:1]
        weight_x = jnp.where(x_rows == 0, 1.0 - frac_x, jnp.where(x_rows == 1, frac_x, 0.0))
        for x in range(CX):
            hat_xy[dg, j, x * CY : (x + 1) * CY] = weight_x[x : x + 1] * weight_y

    def spread(dg, j):
        hats(dg, j)
        weight_xy = hat_xy[dg, j]
        cell = cell_recv[dg, j]
        pushed = jnp.concatenate([weight_xy * cell[4 + d : 5 + d] for d in range(3)], axis=0)
        push_high, push_low = halves(pushed)
        both = dot_nt(jnp.concatenate([push_high, push_low], axis=0), hat_z[dg, j])
        high_rows, low_rows = both[0 : 3 * XY], both[3 * XY :]
        return high_rows[:, 0:NZ] + high_rows[:, NZ : 2 * NZ] + low_rows[:, 0:NZ]

    total = spread(0, 0)

    pl.semaphore_wait(barrier, expected)

    edge_copy = to_pair(edge_send, edge_recv, 0)
    cell_copies = {
        (0, j): pltpu.make_async_remote_copy(
            src_ref=cell_send.at[j],
            dst_ref=cell_recv.at[0, j],
            send_sem=cell_sems.at[0, 0, j],
            recv_sem=cell_sems.at[1, 0, j],
            device_id=(g, s, tile_at[j]),
            device_id_type=MESH,
        )
        for j in (2, 1, 3)
    }
    for copy in cell_copies.values():
        copy.start()
    edge_copy.start()
    late_copies = [
        pltpu.make_async_remote_copy(
            src_ref=cell_send.at[j, 0:4],
            dst_ref=cell_recv.at[1, j, 0:4],
            send_sem=cell_sems.at[0, 1, j],
            recv_sem=cell_sems.at[1, 1, j],
            device_id=(other, s, tile_at[j]),
            device_id_type=MESH,
        )
        for j in range(TILES)
    ]

    z_rows = lax.broadcasted_iota(jnp.int32, (NZ, EDGE), 0)
    put_z = jnp.where(z_rows == (write_sites & (NZ - 1)), 1.0, 0.0).astype(jnp.bfloat16)
    xy_rows = lax.broadcasted_iota(jnp.int32, (XY, EDGE), 0)
    put_xy = jnp.where(xy_rows == (write_sites >> 7), 1.0, 0.0)
    written = dot_nt(put_xy.astype(jnp.bfloat16), put_z).reshape(CX, CY, NZ) > 0.5
    for j in (1, 3, 2):
        cell_copies[0, j].wait_recv()
        total = total + spread(0, j)
    force_send[...] = total.reshape(3, CX, CY, NZ)
    force_copy = to_pair(force_send, force_recv, 2)
    force_copy.start()

    edge_copy.wait_recv()
    for i in range(19):
        row = edge_recv[i : i + 1, :]
        row_high = f32(row.astype(jnp.bfloat16))
        edge_high[i * XY : (i + 1) * XY] = (put_xy * row_high).astype(jnp.bfloat16)
        edge_low[i * XY : (i + 1) * XY] = (put_xy * (row - row_high)).astype(jnp.bfloat16)
    placed = dot_nt(edge_high[...], put_z) + dot_nt(edge_low[...], put_z)
    for i in range(19):
        new = placed[i * XY : (i + 1) * XY].reshape(CX, CY, NZ)
        lat[i] = jnp.where(written, new, lat[i])

    loads[5].wait()
    wet[...] = jnp.where(fluid[...] > 0, 1.0, 0.0)

    force_copy.wait_recv()
    for d in range(3):
        force[d] = force_send[d] + force_recv[d]

    @pl.when(g == 0)
    def _():
        for copy in late_copies:
            copy.start()

    relax = jnp.where(window, tau_fine, tau_coarse)
    inverse = jnp.where(window, 1.0 / tau_fine, 1.0 / tau_coarse)

    y_index = lax.broadcasted_iota(jnp.int32, (CX, CY, NZ), 1)
    z_index = lax.broadcasted_iota(jnp.int32, (CX, CY, NZ), 2)
    x_row = lax.broadcasted_iota(jnp.int32, (CX, NZ), 0)

    def shifted(block, move, low_x, high_x, low_y, high_y, corner):
        a, b, e = move
        if a == 1:
            block = jnp.concatenate([low_x[None], block[:-1]], axis=0)
        elif a == -1:
            block = jnp.concatenate([block[1:], high_x[None]], axis=0)
        if b != 0:
            side = low_y if b == 1 else high_y
            if a == 1:
                side = jnp.where(x_row == 0, corner, pltpu.roll(side, 1, 0))
            elif a == -1:
                side = jnp.where(x_row == CX - 1, corner, pltpu.roll(side, CX - 1, 0))
            block = pltpu.roll(block, 1 if b == 1 else CY - 1, 1)
            side = jnp.broadcast_to(side[:, None, :], (CX, CY, NZ))
            block = jnp.where(y_index == (0 if b == 1 else CY - 1), side, block)
        if e != 0:
            block = pltpu.roll(block, 1 if e == 1 else NZ - 1, 2)
        return block

    def sweep(turn, meanwhile):
        popul = [lat[i] for i in range(19)]
        density, momenta = moments(popul)
        velocity = [(momenta[d] + relax * force[d]) / density for d in range(3)]
        target = equilibrium(density, velocity)
        wet_here = wet[...] > 0.5
        for i in range(19):
            post[i] = jnp.where(wet_here, popul[i] - (popul[i] - target[i]) * inverse, popul[i])
        for k in range(5):
            face_send[turn, 0, k] = post[X_UP[k], CX - 1]
            face_send[turn, 1, k] = post[X_DOWN[k], 0]
            face_send[turn, 2, k] = post[Y_UP[k], :, CY - 1, :]
            face_send[turn, 3, k] = post[Y_DOWN[k], :, 0, :]
        face_send[turn, 0, 5] = wet[CX - 1]
        face_send[turn, 1, 5] = wet[0]
        face_send[turn, 2, 5] = wet[:, CY - 1, :]
        face_send[turn, 3, 5] = wet[:, 0, :]
        for k, i in enumerate(DIAGONAL):
            x = CX - 1 if lattice_c[i][0] == 1 else 0
            y = CY - 1 if lattice_c[i][1] == 1 else 0
            row_send[turn, k, 0:1] = post[i, x, y : y + 1, :]
            row_send[turn, k, 1:2] = wet[x, y : y + 1, :]
        copies = []
        moves = [(1, 0), (-1, 0), (0, 1), (0, -1)]
        for k in range(4):
            copies.append(
                (
                    moves[k],
                    pltpu.make_async_remote_copy(
                        src_ref=face_send.at[turn, k],
                        dst_ref=face_recv.at[turn, k],
                        send_sem=face_sems.at[turn, 0, k],
                        recv_sem=face_sems.at[turn, 1, k],
                        device_id=(g, at_x[moves[k][0]], at_y[moves[k][1]]),
                        device_id_type=MESH,
                    ),
                )
            )
        for k, i in enumerate(DIAGONAL):
            a, b, _ = lattice_c[i]
            copies.append(
                (
                    (a, b),
                    pltpu.make_async_remote_copy(
                        src_ref=row_send.at[turn, k],
                        dst_ref=row_recv.at[turn, k],
                        send_sem=row_sems.at[turn, 0, k],
                        recv_sem=row_sems.at[turn, 1, k],
                        device_id=(g, at_x[a], at_y[b]),
                        device_id_type=MESH,
                    ),
                )
            )
        for (a, b), copy in reversed(copies):
            pl.when(exists(a, b))(copy.start)
        meanwhile()
        for (a, b), copy in copies:
            pl.when(exists(-a, -b))(copy.wait_recv)
        if turn == 0:
            ones = jnp.ones((8, NZ), jnp.int32)

            def known(flags, a, b):
                if a != 0:
                    flags = jnp.where(ones * s != (0 if a == 1 else slabs - 1), flags, 0.0)
                if b != 0:
                    flags = jnp.where(ones * t != (0 if b == 1 else TILES - 1), flags, 0.0)
                return flags

            for i in range(1, 19):
                a, b, e = lattice_c[i]
                corner = None
                if i in DIAGONAL:
                    k = DIAGONAL.index(i)
                    corner = known(jnp.broadcast_to(row_recv[0, k, 1:2], (8, NZ)), a, b)
                moved = shifted(
                    wet[...],
                    lattice_c[i],
                    known(face_recv[0, 0, 5], 1, 0),
                    known(face_recv[0, 1, 5], -1, 0),
                    known(face_recv[0, 2, 5], 0, 1),
                    known(face_recv[0, 3, 5], 0, -1),
                    corner,
                )
                if e != 0:
                    moved = jnp.where(z_index == (0 if e == 1 else NZ - 1), 0.0, moved)
                open_mask[i] = moved
        for i in range(19):
            if i == 0:
                lat[0] = post[0]
                continue
            a, b, e = lattice_c[i]
            moved = shifted(
                post[i],
                lattice_c[i],
                face_recv[turn, 0, X_UP.index(i)] if a == 1 else None,
                face_recv[turn, 1, X_DOWN.index(i)] if a == -1 else None,
                face_recv[turn, 2, Y_UP.index(i)] if b == 1 else None,
                face_recv[turn, 3, Y_DOWN.index(i)] if b == -1 else None,
                row_recv[turn, DIAGONAL.index(i), 0:1] if i in DIAGONAL else None,
            )
            moved = jnp.where(open_mask[i] > 0.5, moved, post[opposite[i]])
            lat[i] = jnp.where(wet_here, moved, post[i])
        for (a, b), copy in copies:
            pl.when(exists(a, b))(copy.wait_send)

    def late_hats():
        for j in range(TILES):
            late_copies[j].wait_recv()
            hats(1, j)

    def half_velocity():
        density, momenta = moments([lat[i] for i in range(19)])
        for d in range(3):
            vel_send[d] = 0.5 * ((momenta[d] + 0.5 * force[d]) / density)

    sweep(0, lambda: None)
    vel_copy = to_pair(vel_send, vel_recv, 1)

    def return_copy(dg, j):
        return pltpu.make_async_remote_copy(
            src_ref=ret_send.at[dg, j],
            dst_ref=ret_recv.at[j],
            send_sem=ret_send_sems.at[dg, j],
            recv_sem=ret_recv_sems.at[j],
            device_id=(other if dg else g, s, tile_at[(TILES - j) % TILES]),
            device_id_type=MESH,
        )

    @pl.when(g == 0)
    def _():
        half_velocity()
        vel_copy.start()
        return_copy(1, 0).wait_recv()
        vel_copy.wait_send()
        for copy in late_copies:
            copy.wait_send()

    @pl.when(window)
    def _():
        sweep(1, late_hats)
        half_velocity()
        vel_copy.wait_recv()
        speed = (vel_send[...] + vel_recv[...]).reshape(3 * XY, NZ)
        speed_high, speed_low = halves(speed)
        speed_twice = jnp.concatenate([speed_high, speed_high], axis=1)
        for dg, j in ((1, 2), (1, 1), (1, 3), (1, 0), (0, 2), (0, 1), (0, 3), (0, 0)):
            seen = dot_nn(speed_twice, hat_z[dg, j]) + dot_nn(speed_low, hat_z[dg, j, 0:NZ])
            for d in range(3):
                reading = jnp.sum(
                    seen[d * XY : (d + 1) * XY] * hat_xy[dg, j], axis=0, keepdims=True
                )
                if dg + j > 0:
                    ret_send[dg, j, d : d + 1] = reading
                else:
                    ret_recv[0, d : d + 1] = reading
            if dg + j > 0:
                return_copy(dg, j).start()
        for dg in range(2):
            for j in range(TILES):
                if dg + j > 0:
                    return_copy(dg, j).wait_send()

    for j in range(1, TILES):
        return_copy(0, j).wait_recv()
    for c in range(CELLS):
        value = None
        for j in range(TILES):
            for k in range(CAP):
                term = chosen(j, k, c) * ret_recv[j, :, k * PAD : (k + 1) * PAD]
                value = term if value is None else value + term
        for d in range(3):
            out_vel[d, c : c + 1] = value[d : d + 1, 0:VERTS]

    for copy in cell_copies.values():
        copy.wait_send()
    edge_copy.wait_send()
    force_copy.wait_send()


def local(populations, fluid, couple, owner, vertex_site, frac, ref_shape):
    hbm = pl.BlockSpec(memory_space=pl.ANY)
    vmem = pl.BlockSpec(memory_space=pltpu.VMEM)
    real = jnp.float32
    half = jnp.bfloat16
    new, velocity = pl.pallas_call(
        kernel,
        out_shape=(
            pltpu.VMEM(populations.shape, real),
            pltpu.VMEM((3, CELLS, VERTS), real),
        ),
        in_specs=[hbm, hbm, hbm, pl.BlockSpec(memory_space=pltpu.SMEM), hbm, hbm, hbm],
        out_specs=(vmem, vmem),
        scratch_shapes=[
            pltpu.VMEM((CX, CY, NZ), jnp.int32),
            pltpu.VMEM((2, 1, EDGE), jnp.int32),
            pltpu.VMEM((CELLS, VERTS), jnp.int32),
            pltpu.VMEM((3, CELLS, VERTS), real),
            pltpu.VMEM((3, CELLS, VERTS), real),
            pltpu.VMEM((CELLS, 8, PAD), real),
            pltpu.VMEM((TILES, 8, WIDE), real),
            pltpu.VMEM((2, TILES, 8, WIDE), real),
            pltpu.VMEM((19 * XY, 2 * NZ), half),
            pltpu.VMEM((19, EDGE), real),
            pltpu.VMEM((19, EDGE), real),
            pltpu.VMEM((19 * XY, EDGE), half),
            pltpu.VMEM((19 * XY, EDGE), half),
            pltpu.VMEM((2, TILES, XY, WIDE), real),
            pltpu.VMEM((2, TILES, 2 * NZ, WIDE), half),
            pltpu.VMEM((3, CX, CY, NZ), real),
            pltpu.VMEM((3, CX, CY, NZ), real),
            pltpu.VMEM((3, CX, CY, NZ), real),
            pltpu.VMEM((19, CX, CY, NZ), real),
            pltpu.VMEM((CX, CY, NZ), real),
            pltpu.VMEM((19, CX, CY, NZ), real),
            pltpu.VMEM((2, 4, 6, 8, NZ), real),
            pltpu.VMEM((2, 4, 6, 8, NZ), real),
            pltpu.VMEM((2, 4, 2, NZ), real),
            pltpu.VMEM((2, 4, 2, NZ), real),
            pltpu.VMEM((3, CX, CY, NZ), real),
            pltpu.VMEM((3, CX, CY, NZ), real),
            pltpu.VMEM((2, TILES, 3, WIDE), real),
            pltpu.VMEM((TILES, 3, WIDE), real),
            pltpu.SemaphoreType.DMA((6,)),
            pltpu.SemaphoreType.DMA((2, 2, TILES)),
            pltpu.SemaphoreType.DMA((2, 3)),
            pltpu.SemaphoreType.DMA((2, 2, 4)),
            pltpu.SemaphoreType.DMA((2, 2, 4)),
            pltpu.SemaphoreType.DMA((2, TILES)),
            pltpu.SemaphoreType.DMA((TILES,)),
        ],
        compiler_params=pltpu.CompilerParams(
            collective_id=0, has_side_effects=True, vmem_limit_bytes=62 * 2**20
        ),
    )(
        populations,
        fluid,
        couple.reshape(2, 1, EDGE),
        owner.reshape(CELLS),
        vertex_site,
        jnp.transpose(frac, (1, 0, 2)),
        jnp.transpose(ref_shape, (1, 0, 2)),
    )
    return new, jnp.transpose(velocity, (1, 0, 2))


def solution(mesh):
    return jax.shard_map(
        local,
        mesh=mesh,
        in_specs=(
            P("group", None, "slab", "tile", None),
            P("group", "slab", "tile", None),
            P("group", "slab", "tile", None),
            P(("group", "slab", "tile"), None),
            P(("group", "slab", "tile"), None),
            P(("group", "slab", "tile"), None, None),
            P(("group", "slab", "tile"), None, None),
        ),
        out_specs=(
            P("group", None, "slab", "tile", None),
            P(("group", "slab", "tile"), None, None),
        ),
        check_vma=False,
    )
```

```python
import jax
import jax.numpy as jnp
from jax import lax
from jax.experimental import pallas as pl
from jax.experimental.pallas import tpu as pltpu
from jax.sharding import PartitionSpec as P

MESH = pl.DeviceIdType.MESH
CX = 8
CY = 8
NZ = 128
XY = CX * CY
VERTS = 642
PAD = 768
WIDE = 2 * PAD
CELLS = 4
CAP = 2
EDGE = 1024
TILES = 4

lattice_c = [
    (0, 0, 0),
    (1, 0, 0),
    (-1, 0, 0),
    (0, 1, 0),
    (0, -1, 0),
    (0, 0, 1),
    (0, 0, -1),
    (1, 1, 0),
    (-1, -1, 0),
    (1, -1, 0),
    (-1, 1, 0),
    (1, 0, 1),
    (-1, 0, -1),
    (1, 0, -1),
    (-1, 0, 1),
    (0, 1, 1),
    (0, -1, -1),
    (0, 1, -1),
    (0, -1, 1),
]
lattice_w = [1.0 / 3.0] + [1.0 / 18.0] * 6 + [1.0 / 36.0] * 12
opposite = [0, 2, 1, 4, 3, 6, 5, 8, 7, 10, 9, 12, 11, 14, 13, 16, 15, 18, 17]
tau_coarse = 0.8
tau_fine = 1.1
stiffness = 0.01

X_UP = [i for i in range(19) if lattice_c[i][0] == 1]
X_DOWN = [i for i in range(19) if lattice_c[i][0] == -1]
Y_UP = [i for i in range(19) if lattice_c[i][1] == 1]
Y_DOWN = [i for i in range(19) if lattice_c[i][1] == -1]
DIAGONAL = [7, 8, 9, 10]


def f32(x):
    return x.astype(jnp.float32)


def halves(x):
    high = x.astype(jnp.bfloat16)
    low = (x - f32(high)).astype(jnp.bfloat16)
    return high, low


def dot_nn(a, b):
    return lax.dot_general(a, b, (((1,), (0,)), ((), ())), preferred_element_type=jnp.float32)


def dot_nt(a, b):
    return lax.dot_general(a, b, (((1,), (1,)), ((), ())), preferred_element_type=jnp.float32)


def moments(popul):
    density = popul[0]
    momenta = [None, None, None]
    for i in range(1, 19):
        density = density + popul[i]
        for d in range(3):
            sign = lattice_c[i][d]
            if sign == 0:
                continue
            if momenta[d] is None:
                momenta[d] = popul[i]
            elif sign > 0:
                momenta[d] = momenta[d] + popul[i]
            else:
                momenta[d] = momenta[d] - popul[i]
    return density, momenta


def equilibrium(density, velocity):
    ux, uy, uz = velocity
    base = 1.0 - 1.5 * (ux * ux + uy * uy + uz * uz)
    terms = [None] * 19
    terms[0] = lattice_w[0] * density * base
    for i in range(1, 19, 2):
        along = None
        for d in range(3):
            sign = lattice_c[i][d]
            if sign == 0:
                continue
            if along is None:
                along = velocity[d]
            elif sign > 0:
                along = along + velocity[d]
            else:
                along = along - velocity[d]
        weight = lattice_w[i] * density
        even = base + 4.5 * along * along
        odd = 3.0 * along
        terms[i] = weight * (even + odd)
        terms[i + 1] = weight * (even - odd)
    return terms


def kernel(
    pop_hbm,
    fluid_hbm,
    couple_hbm,
    owner_ref,
    site_hbm,
    frac_hbm,
    shape_hbm,
    out_pop,
    out_vel,
    fluid,
    couple,
    site,
    frac,
    rest,
    payload,
    cell_send,
    cell_recv,
    pop_half,
    edge_send,
    edge_recv,
    edge_high,
    edge_low,
    hat_xy,
    hat_z,
    force_send,
    force_recv,
    force,
    post,
    wet,
    open_mask,
    face_send,
    face_recv,
    row_send,
    row_recv,
    vel_send,
    vel_recv,
    ret_send,
    ret_recv,
    in_sem,
    cell_sems,
    pair_sems,
    face_sems,
    row_sems,
    ret_send_sems,
    ret_recv_sems,
    ready,
):
    lat = out_pop.at[0]
    g = lax.axis_index("group")
    s = lax.axis_index("slab")
    t = lax.axis_index("tile")
    slabs = lax.axis_size("slab")
    window = g == 1
    up_s, down_s = lax.rem(s + 1, slabs), lax.rem(s + slabs - 1, slabs)
    tile_at = [lax.rem(t + j, TILES) for j in range(TILES)]
    other = 1 - g
    has_x = {1: s < slabs - 1, -1: s > 0}
    has_y = {1: t < TILES - 1, -1: t > 0, 0: t >= 0}
    at_x = {1: up_s, -1: down_s, 0: s}
    at_y = {1: tile_at[1], -1: tile_at[3], 0: t}

    def exists(a, b):
        if a == 0:
            return has_y[b]
        if b == 0:
            return has_x[a]
        return has_x[a] & has_y[b]

    barrier = pltpu.get_barrier_semaphore()
    seam = slabs // 2
    greets = {1: (s < slabs - 1) & (s != seam - 1), -1: s == seam}
    greeted = {-1: (s > 0) & (s != seam), 1: s == seam - 1}
    per_side = 1 + jnp.where(has_y[1], 1, 0) + jnp.where(has_y[-1], 1, 0)

    def to_side(semaphore, sides):
        for a in (1, -1):
            for b in (0, 1, -1):

                @pl.when(sides[a] & has_y[b])
                def _():
                    pl.semaphore_signal(
                        semaphore,
                        inc=1,
                        device_id=(g, at_x[a], at_y[b]),
                        device_id_type=MESH,
                    )

    def from_side(sides):
        return per_side * (jnp.where(sides[1], 1, 0) + jnp.where(sides[-1], 1, 0))

    to_side(barrier, greets)
    for dg in range(2):
        for j in range(TILES):
            if dg + j > 0:
                pl.semaphore_signal(
                    barrier,
                    inc=1,
                    device_id=(other if dg else g, s, tile_at[j]),
                    device_id_type=MESH,
                )

    loads = [
        pltpu.make_async_copy(src, dst, in_sem.at[k])
        for k, (src, dst) in enumerate(
            [
                (site_hbm, site),
                (frac_hbm, frac),
                (shape_hbm, rest),
                (couple_hbm, couple),
                (pop_hbm.at[0], lat),
                (fluid_hbm.at[0], fluid),
            ]
        )
    ]
    for load in loads:
        load.start()

    payload[...] = jnp.zeros_like(payload)
    for load in loads[:3]:
        load.wait()
    site_value = site[...]
    coords = [
        site_value >> 10,
        (site_value >> 7) & (CY - 1),
        site_value & (NZ - 1),
    ]
    for d in range(3):
        offset = frac[d]
        position = f32(coords[d]) + offset
        centre = jnp.sum(position, axis=1, keepdims=True) * (1.0 / VERTS)
        push = -stiffness * (position - centre - rest[d])
        for c in range(CELLS):
            payload[c, d : d + 1, 0:VERTS] = offset[c : c + 1]
            payload[c, 4 + d : 5 + d, 0:VERTS] = push[c : c + 1]
    for c in range(CELLS):
        payload[c, 3:4, 0:VERTS] = f32(site_value[c : c + 1])

    owners = [owner_ref[c] for c in range(CELLS)]
    ranks = []
    for c in range(CELLS):
        rank = jnp.int32(0)
        for before in range(c):
            rank = rank + jnp.where(owners[before] == owners[c], 1, 0)
        ranks.append(rank)

    def chosen(j, k, c):
        return jnp.where((owners[c] == tile_at[j]) & (ranks[c] == k), 1.0, 0.0)

    for j in range(TILES):
        for k in range(CAP):
            slot = chosen(j, k, 0) * payload[0]
            for c in range(1, CELLS):
                slot = slot + chosen(j, k, c) * payload[c]
            cell_send[j, :, k * PAD : (k + 1) * PAD] = slot
            if j == 0:
                cell_recv[0, 0, :, k * PAD : (k + 1) * PAD] = slot

    def to_pair(src, dst, k):
        return pltpu.make_async_remote_copy(
            src_ref=src,
            dst_ref=dst,
            send_sem=pair_sems.at[0, k],
            recv_sem=pair_sems.at[1, k],
            device_id=(other, s, t),
            device_id_type=MESH,
        )

    loads[3].wait()
    loads[4].wait()
    row_0, row_1 = couple[0], couple[1]
    read_sites = row_0 + g * (row_1 - row_0)
    write_sites = row_1 + g * (row_0 - row_1)
    high, low = halves(lat[...].reshape(19 * XY, NZ))
    pop_half[:, 0:NZ] = high
    pop_half[:, NZ : 2 * NZ] = low
    chunk = 256
    for k in range(EDGE // chunk):
        sites = read_sites[:, k * chunk : (k + 1) * chunk]
        z_rows = lax.broadcasted_iota(jnp.int32, (NZ, chunk), 0)
        pick_z = jnp.where(z_rows == (sites & (NZ - 1)), 1.0, 0.0).astype(jnp.bfloat16)
        pick_z = jnp.concatenate([pick_z, pick_z], axis=0)
        xy_rows = lax.broadcasted_iota(jnp.int32, (XY, chunk), 0)
        pick_xy = jnp.where(xy_rows == (sites >> 7), 1.0, 0.0)
        found = dot_nn(pop_half[...], pick_z)
        for i in range(19):
            edge_send[i : i + 1, k * chunk : (k + 1) * chunk] = jnp.sum(
                found[i * XY : (i + 1) * XY] * pick_xy, axis=0, keepdims=True
            )
    rows = [edge_send[i : i + 1, :] for i in range(19)]
    density, momenta = moments(rows)
    target = equilibrium(density, [m / density for m in momenta])
    factor = jnp.where(window, 2.0 * tau_coarse / tau_fine, tau_fine / (2.0 * tau_coarse))
    for i in range(19):
        edge_send[i : i + 1, :] = target[i] + factor * (rows[i] - target[i])

    def hats(dg, j):
        cell = cell_recv[dg, j, 0:4]
        where_at = cell[3:4].astype(jnp.int32)
        z_rows = lax.broadcasted_iota(jnp.int32, (NZ, WIDE), 0) - (where_at & (NZ - 1))
        frac_z = cell[2:3]
        weight_z = jnp.where(z_rows == 0, 1.0 - frac_z, jnp.where(z_rows == 1, frac_z, 0.0))
        z_high, z_low = halves(weight_z)
        hat_z[dg, j, 0:NZ] = z_high
        hat_z[dg, j, NZ : 2 * NZ] = z_low
        y_rows = lax.broadcasted_iota(jnp.int32, (CY, WIDE), 0) - ((where_at >> 7) & (CY - 1))
        frac_y = cell[1:2]
        weight_y = jnp.where(y_rows == 0, 1.0 - frac_y, jnp.where(y_rows == 1, frac_y, 0.0))
        x_rows = lax.broadcasted_iota(jnp.int32, (CX, WIDE), 0) - (where_at >> 10)
        frac_x = cell[0:1]
        weight_x = jnp.where(x_rows == 0, 1.0 - frac_x, jnp.where(x_rows == 1, frac_x, 0.0))
        for x in range(CX):
            hat_xy[dg, j, x * CY : (x + 1) * CY] = weight_x[x : x + 1] * weight_y

    def spread(dg, j):
        hats(dg, j)
        weight_xy = hat_xy[dg, j]
        cell = cell_recv[dg, j]
        pushed = jnp.concatenate([weight_xy * cell[4 + d : 5 + d] for d in range(3)], axis=0)
        push_high, push_low = halves(pushed)
        both = dot_nt(jnp.concatenate([push_high, push_low], axis=0), hat_z[dg, j])
        high_rows, low_rows = both[0 : 3 * XY], both[3 * XY :]
        return high_rows[:, 0:NZ] + high_rows[:, NZ : 2 * NZ] + low_rows[:, 0:NZ]

    total = spread(0, 0)

    pl.semaphore_wait(barrier, 2 * TILES - 1 + from_side(greeted))

    edge_copy = to_pair(edge_send, edge_recv, 0)
    cell_copies = {
        (0, j): pltpu.make_async_remote_copy(
            src_ref=cell_send.at[j],
            dst_ref=cell_recv.at[0, j],
            send_sem=cell_sems.at[0, 0, j],
            recv_sem=cell_sems.at[1, 0, j],
            device_id=(g, s, tile_at[j]),
            device_id_type=MESH,
        )
        for j in (2, 1, 3)
    }
    for copy in cell_copies.values():
        copy.start()
    edge_copy.start()
    to_side(ready, greeted)
    late_copies = [
        pltpu.make_async_remote_copy(
            src_ref=cell_send.at[j, 0:4],
            dst_ref=cell_recv.at[1, j, 0:4],
            send_sem=cell_sems.at[0, 1, j],
            recv_sem=cell_sems.at[1, 1, j],
            device_id=(other, s, tile_at[j]),
            device_id_type=MESH,
        )
        for j in range(TILES)
    ]

    z_rows = lax.broadcasted_iota(jnp.int32, (NZ, EDGE), 0)
    put_z = jnp.where(z_rows == (write_sites & (NZ - 1)), 1.0, 0.0).astype(jnp.bfloat16)
    xy_rows = lax.broadcasted_iota(jnp.int32, (XY, EDGE), 0)
    put_xy = jnp.where(xy_rows == (write_sites >> 7), 1.0, 0.0)
    written = dot_nt(put_xy.astype(jnp.bfloat16), put_z).reshape(CX, CY, NZ) > 0.5
    for j in (1, 3, 2):
        cell_copies[0, j].wait_recv()
        total = total + spread(0, j)
    force_send[...] = total.reshape(3, CX, CY, NZ)
    force_copy = to_pair(force_send, force_recv, 2)
    force_copy.start()

    edge_copy.wait_recv()
    for i in range(19):
        row = edge_recv[i : i + 1, :]
        row_high = f32(row.astype(jnp.bfloat16))
        edge_high[i * XY : (i + 1) * XY] = (put_xy * row_high).astype(jnp.bfloat16)
        edge_low[i * XY : (i + 1) * XY] = (put_xy * (row - row_high)).astype(jnp.bfloat16)
    placed = dot_nt(edge_high[...], put_z) + dot_nt(edge_low[...], put_z)
    for i in range(19):
        new = placed[i * XY : (i + 1) * XY].reshape(CX, CY, NZ)
        lat[i] = jnp.where(written, new, lat[i])

    loads[5].wait()
    wet[...] = jnp.where(fluid[...] > 0, 1.0, 0.0)

    force_copy.wait_recv()
    for d in range(3):
        force[d] = force_send[d] + force_recv[d]

    @pl.when(g == 0)
    def _():
        for copy in late_copies:
            copy.start()

    relax = jnp.where(window, tau_fine, tau_coarse)
    inverse = jnp.where(window, 1.0 / tau_fine, 1.0 / tau_coarse)

    y_index = lax.broadcasted_iota(jnp.int32, (CX, CY, NZ), 1)
    z_index = lax.broadcasted_iota(jnp.int32, (CX, CY, NZ), 2)
    x_row = lax.broadcasted_iota(jnp.int32, (CX, NZ), 0)

    def shifted(block, move, low_x, high_x, low_y, high_y, corner):
        a, b, e = move
        if a == 1:
            block = jnp.concatenate([low_x[None], block[:-1]], axis=0)
        elif a == -1:
            block = jnp.concatenate([block[1:], high_x[None]], axis=0)
        if b != 0:
            side = low_y if b == 1 else high_y
            if a == 1:
                side = jnp.where(x_row == 0, corner, pltpu.roll(side, 1, 0))
            elif a == -1:
                side = jnp.where(x_row == CX - 1, corner, pltpu.roll(side, CX - 1, 0))
            block = pltpu.roll(block, 1 if b == 1 else CY - 1, 1)
            side = jnp.broadcast_to(side[:, None, :], (CX, CY, NZ))
            block = jnp.where(y_index == (0 if b == 1 else CY - 1), side, block)
        if e != 0:
            block = pltpu.roll(block, 1 if e == 1 else NZ - 1, 2)
        return block

    def sweep(turn, meanwhile):
        popul = [lat[i] for i in range(19)]
        density, momenta = moments(popul)
        velocity = [(momenta[d] + relax * force[d]) / density for d in range(3)]
        target = equilibrium(density, velocity)
        wet_here = wet[...] > 0.5
        for i in range(19):
            post[i] = jnp.where(wet_here, popul[i] - (popul[i] - target[i]) * inverse, popul[i])
        for k in range(5):
            face_send[turn, 0, k] = post[X_UP[k], CX - 1]
            face_send[turn, 1, k] = post[X_DOWN[k], 0]
            face_send[turn, 2, k] = post[Y_UP[k], :, CY - 1, :]
            face_send[turn, 3, k] = post[Y_DOWN[k], :, 0, :]
        face_send[turn, 0, 5] = wet[CX - 1]
        face_send[turn, 1, 5] = wet[0]
        face_send[turn, 2, 5] = wet[:, CY - 1, :]
        face_send[turn, 3, 5] = wet[:, 0, :]
        for k, i in enumerate(DIAGONAL):
            x = CX - 1 if lattice_c[i][0] == 1 else 0
            y = CY - 1 if lattice_c[i][1] == 1 else 0
            row_send[turn, k, 0:1] = post[i, x, y : y + 1, :]
            row_send[turn, k, 1:2] = wet[x, y : y + 1, :]
        copies = []
        moves = [(1, 0), (-1, 0), (0, 1), (0, -1)]
        for k in range(4):
            copies.append(
                (
                    moves[k],
                    pltpu.make_async_remote_copy(
                        src_ref=face_send.at[turn, k],
                        dst_ref=face_recv.at[turn, k],
                        send_sem=face_sems.at[turn, 0, k],
                        recv_sem=face_sems.at[turn, 1, k],
                        device_id=(g, at_x[moves[k][0]], at_y[moves[k][1]]),
                        device_id_type=MESH,
                    ),
                )
            )
        for k, i in enumerate(DIAGONAL):
            a, b, _ = lattice_c[i]
            copies.append(
                (
                    (a, b),
                    pltpu.make_async_remote_copy(
                        src_ref=row_send.at[turn, k],
                        dst_ref=row_recv.at[turn, k],
                        send_sem=row_sems.at[turn, 0, k],
                        recv_sem=row_sems.at[turn, 1, k],
                        device_id=(g, at_x[a], at_y[b]),
                        device_id_type=MESH,
                    ),
                )
            )
        if turn == 0:

            @pl.when(greets[1] | greets[-1])
            def _():
                pl.semaphore_wait(ready, from_side(greets))

        for (a, b), copy in reversed(copies):
            pl.when(exists(a, b))(copy.start)
        meanwhile()
        for (a, b), copy in copies:
            pl.when(exists(-a, -b))(copy.wait_recv)
        if turn == 0:
            ones = jnp.ones((8, NZ), jnp.int32)

            def known(flags, a, b):
                if a != 0:
                    flags = jnp.where(ones * s != (0 if a == 1 else slabs - 1), flags, 0.0)
                if b != 0:
                    flags = jnp.where(ones * t != (0 if b == 1 else TILES - 1), flags, 0.0)
                return flags

            for i in range(1, 19):
                a, b, e = lattice_c[i]
                corner = None
                if i in DIAGONAL:
                    k = DIAGONAL.index(i)
                    corner = known(jnp.broadcast_to(row_recv[0, k, 1:2], (8, NZ)), a, b)
                moved = shifted(
                    wet[...],
                    lattice_c[i],
                    known(face_recv[0, 0, 5], 1, 0),
                    known(face_recv[0, 1, 5], -1, 0),
                    known(face_recv[0, 2, 5], 0, 1),
                    known(face_recv[0, 3, 5], 0, -1),
                    corner,
                )
                if e != 0:
                    moved = jnp.where(z_index == (0 if e == 1 else NZ - 1), 0.0, moved)
                open_mask[i] = moved
        for i in range(19):
            if i == 0:
                lat[0] = post[0]
                continue
            a, b, e = lattice_c[i]
            moved = shifted(
                post[i],
                lattice_c[i],
                face_recv[turn, 0, X_UP.index(i)] if a == 1 else None,
                face_recv[turn, 1, X_DOWN.index(i)] if a == -1 else None,
                face_recv[turn, 2, Y_UP.index(i)] if b == 1 else None,
                face_recv[turn, 3, Y_DOWN.index(i)] if b == -1 else None,
                row_recv[turn, DIAGONAL.index(i), 0:1] if i in DIAGONAL else None,
            )
            moved = jnp.where(open_mask[i] > 0.5, moved, post[opposite[i]])
            lat[i] = jnp.where(wet_here, moved, post[i])
        for (a, b), copy in copies:
            pl.when(exists(a, b))(copy.wait_send)

    def late_hats():
        for j in range(TILES):
            late_copies[j].wait_recv()
            hats(1, j)

    def half_velocity():
        density, momenta = moments([lat[i] for i in range(19)])
        for d in range(3):
            vel_send[d] = 0.5 * ((momenta[d] + 0.5 * force[d]) / density)

    sweep(0, lambda: None)
    vel_copy = to_pair(vel_send, vel_recv, 1)

    def return_copy(dg, j):
        return pltpu.make_async_remote_copy(
            src_ref=ret_send.at[dg, j],
            dst_ref=ret_recv.at[j],
            send_sem=ret_send_sems.at[dg, j],
            recv_sem=ret_recv_sems.at[j],
            device_id=(other if dg else g, s, tile_at[(TILES - j) % TILES]),
            device_id_type=MESH,
        )

    @pl.when(g == 0)
    def _():
        half_velocity()
        vel_copy.start()
        return_copy(1, 0).wait_recv()
        vel_copy.wait_send()
        for copy in late_copies:
            copy.wait_send()

    @pl.when(window)
    def _():
        sweep(1, late_hats)
        half_velocity()
        vel_copy.wait_recv()
        speed = (vel_send[...] + vel_recv[...]).reshape(3 * XY, NZ)
        speed_high, speed_low = halves(speed)
        speed_twice = jnp.concatenate([speed_high, speed_high], axis=1)
        for dg, j in ((1, 2), (1, 1), (1, 3), (1, 0), (0, 2), (0, 1), (0, 3), (0, 0)):
            seen = dot_nn(speed_twice, hat_z[dg, j]) + dot_nn(speed_low, hat_z[dg, j, 0:NZ])
            for d in range(3):
                reading = jnp.sum(
                    seen[d * XY : (d + 1) * XY] * hat_xy[dg, j], axis=0, keepdims=True
                )
                if dg + j > 0:
                    ret_send[dg, j, d : d + 1] = reading
                else:
                    ret_recv[0, d : d + 1] = reading
            if dg + j > 0:
                return_copy(dg, j).start()
        for dg in range(2):
            for j in range(TILES):
                if dg + j > 0:
                    return_copy(dg, j).wait_send()

    for j in range(1, TILES):
        return_copy(0, j).wait_recv()
    for c in range(CELLS):
        value = None
        for j in range(TILES):
            for k in range(CAP):
                term = chosen(j, k, c) * ret_recv[j, :, k * PAD : (k + 1) * PAD]
                value = term if value is None else value + term
        for d in range(3):
            out_vel[d, c : c + 1] = value[d : d + 1, 0:VERTS]

    for copy in cell_copies.values():
        copy.wait_send()
    edge_copy.wait_send()
    force_copy.wait_send()


def local(populations, fluid, couple, owner, vertex_site, frac, ref_shape):
    hbm = pl.BlockSpec(memory_space=pl.ANY)
    vmem = pl.BlockSpec(memory_space=pltpu.VMEM)
    real = jnp.float32
    half = jnp.bfloat16
    new, velocity = pl.pallas_call(
        kernel,
        out_shape=(
            pltpu.VMEM(populations.shape, real),
            pltpu.VMEM((3, CELLS, VERTS), real),
        ),
        in_specs=[hbm, hbm, hbm, pl.BlockSpec(memory_space=pltpu.SMEM), hbm, hbm, hbm],
        out_specs=(vmem, vmem),
        scratch_shapes=[
            pltpu.VMEM((CX, CY, NZ), jnp.int32),
            pltpu.VMEM((2, 1, EDGE), jnp.int32),
            pltpu.VMEM((CELLS, VERTS), jnp.int32),
            pltpu.VMEM((3, CELLS, VERTS), real),
            pltpu.VMEM((3, CELLS, VERTS), real),
            pltpu.VMEM((CELLS, 8, PAD), real),
            pltpu.VMEM((TILES, 8, WIDE), real),
            pltpu.VMEM((2, TILES, 8, WIDE), real),
            pltpu.VMEM((19 * XY, 2 * NZ), half),
            pltpu.VMEM((19, EDGE), real),
            pltpu.VMEM((19, EDGE), real),
            pltpu.VMEM((19 * XY, EDGE), half),
            pltpu.VMEM((19 * XY, EDGE), half),
            pltpu.VMEM((2, TILES, XY, WIDE), real),
            pltpu.VMEM((2, TILES, 2 * NZ, WIDE), half),
            pltpu.VMEM((3, CX, CY, NZ), real),
            pltpu.VMEM((3, CX, CY, NZ), real),
            pltpu.VMEM((3, CX, CY, NZ), real),
            pltpu.VMEM((19, CX, CY, NZ), real),
            pltpu.VMEM((CX, CY, NZ), real),
            pltpu.VMEM((19, CX, CY, NZ), real),
            pltpu.VMEM((2, 4, 6, 8, NZ), real),
            pltpu.VMEM((2, 4, 6, 8, NZ), real),
            pltpu.VMEM((2, 4, 2, NZ), real),
            pltpu.VMEM((2, 4, 2, NZ), real),
            pltpu.VMEM((3, CX, CY, NZ), real),
            pltpu.VMEM((3, CX, CY, NZ), real),
            pltpu.VMEM((2, TILES, 3, WIDE), real),
            pltpu.VMEM((TILES, 3, WIDE), real),
            pltpu.SemaphoreType.DMA((6,)),
            pltpu.SemaphoreType.DMA((2, 2, TILES)),
            pltpu.SemaphoreType.DMA((2, 3)),
            pltpu.SemaphoreType.DMA((2, 2, 4)),
            pltpu.SemaphoreType.DMA((2, 2, 4)),
            pltpu.SemaphoreType.DMA((2, TILES)),
            pltpu.SemaphoreType.DMA((TILES,)),
            pltpu.SemaphoreType.REGULAR,
        ],
        compiler_params=pltpu.CompilerParams(
            collective_id=0, has_side_effects=True, vmem_limit_bytes=62 * 2**20
        ),
    )(
        populations,
        fluid,
        couple.reshape(2, 1, EDGE),
        owner.reshape(CELLS),
        vertex_site,
        jnp.transpose(frac, (1, 0, 2)),
        jnp.transpose(ref_shape, (1, 0, 2)),
    )
    return new, jnp.transpose(velocity, (1, 0, 2))


def solution(mesh):
    return jax.shard_map(
        local,
        mesh=mesh,
        in_specs=(
            P("group", None, "slab", "tile", None),
            P("group", "slab", "tile", None),
            P("group", "slab", "tile", None),
            P(("group", "slab", "tile"), None),
            P(("group", "slab", "tile"), None),
            P(("group", "slab", "tile"), None, None),
            P(("group", "slab", "tile"), None, None),
        ),
        out_specs=(
            P("group", None, "slab", "tile", None),
            P(("group", "slab", "tile"), None, None),
        ),
        check_vma=False,
    )
```

```python
import jax
import jax.numpy as jnp
from jax import lax
from jax.experimental import pallas as pl
from jax.experimental.pallas import tpu as pltpu
from jax.sharding import PartitionSpec as P

MESH = pl.DeviceIdType.MESH
CX = 8
CY = 8
NZ = 128
XY = CX * CY
VERTS = 642
PAD = 768
WIDE = 2 * PAD
CELLS = 4
CAP = 2
EDGE = 1024
TILES = 4

lattice_c = [
    (0, 0, 0),
    (1, 0, 0),
    (-1, 0, 0),
    (0, 1, 0),
    (0, -1, 0),
    (0, 0, 1),
    (0, 0, -1),
    (1, 1, 0),
    (-1, -1, 0),
    (1, -1, 0),
    (-1, 1, 0),
    (1, 0, 1),
    (-1, 0, -1),
    (1, 0, -1),
    (-1, 0, 1),
    (0, 1, 1),
    (0, -1, -1),
    (0, 1, -1),
    (0, -1, 1),
]
lattice_w = [1.0 / 3.0] + [1.0 / 18.0] * 6 + [1.0 / 36.0] * 12
opposite = [0, 2, 1, 4, 3, 6, 5, 8, 7, 10, 9, 12, 11, 14, 13, 16, 15, 18, 17]
tau_coarse = 0.8
tau_fine = 1.1
stiffness = 0.01

X_UP = [i for i in range(19) if lattice_c[i][0] == 1]
X_DOWN = [i for i in range(19) if lattice_c[i][0] == -1]
Y_UP = [i for i in range(19) if lattice_c[i][1] == 1]
Y_DOWN = [i for i in range(19) if lattice_c[i][1] == -1]
DIAGONAL = [7, 8, 9, 10]


def f32(x):
    return x.astype(jnp.float32)


def halves(x):
    high = x.astype(jnp.bfloat16)
    low = (x - f32(high)).astype(jnp.bfloat16)
    return high, low


def dot_nn(a, b):
    return lax.dot_general(a, b, (((1,), (0,)), ((), ())), preferred_element_type=jnp.float32)


def dot_nt(a, b):
    return lax.dot_general(a, b, (((1,), (1,)), ((), ())), preferred_element_type=jnp.float32)


def moments(popul):
    density = popul[0]
    momenta = [None, None, None]
    for i in range(1, 19):
        density = density + popul[i]
        for d in range(3):
            sign = lattice_c[i][d]
            if sign == 0:
                continue
            if momenta[d] is None:
                momenta[d] = popul[i]
            elif sign > 0:
                momenta[d] = momenta[d] + popul[i]
            else:
                momenta[d] = momenta[d] - popul[i]
    return density, momenta


def equilibrium(density, velocity):
    ux, uy, uz = velocity
    base = 1.0 - 1.5 * (ux * ux + uy * uy + uz * uz)
    terms = [None] * 19
    terms[0] = lattice_w[0] * density * base
    for i in range(1, 19, 2):
        along = None
        for d in range(3):
            sign = lattice_c[i][d]
            if sign == 0:
                continue
            if along is None:
                along = velocity[d]
            elif sign > 0:
                along = along + velocity[d]
            else:
                along = along - velocity[d]
        weight = lattice_w[i] * density
        even = base + 4.5 * along * along
        odd = 3.0 * along
        terms[i] = weight * (even + odd)
        terms[i + 1] = weight * (even - odd)
    return terms


def kernel(
    pop_hbm,
    fluid_hbm,
    couple_hbm,
    owner_ref,
    site_hbm,
    frac_hbm,
    shape_hbm,
    out_pop,
    out_vel,
    fluid,
    couple,
    site,
    frac,
    rest,
    payload,
    cell_send,
    cell_recv,
    pop_half,
    edge_send,
    edge_recv,
    edge_high,
    edge_low,
    hat_xy,
    hat_z,
    force_send,
    force_recv,
    force,
    post,
    wet,
    open_mask,
    face_send,
    face_recv,
    row_send,
    row_recv,
    vel_send,
    vel_recv,
    ret_send,
    ret_recv,
    in_sem,
    cell_sems,
    pair_sems,
    face_sems,
    row_sems,
    ret_send_sems,
    ret_recv_sems,
    ready,
):
    lat = out_pop.at[0]
    g = lax.axis_index("group")
    s = lax.axis_index("slab")
    t = lax.axis_index("tile")
    slabs = lax.axis_size("slab")
    window = g == 1
    up_s, down_s = lax.rem(s + 1, slabs), lax.rem(s + slabs - 1, slabs)
    tile_at = [lax.rem(t + j, TILES) for j in range(TILES)]
    other = 1 - g
    has_x = {1: s < slabs - 1, -1: s > 0}
    has_y = {1: t < TILES - 1, -1: t > 0, 0: t >= 0}
    at_x = {1: up_s, -1: down_s, 0: s}
    at_y = {1: tile_at[1], -1: tile_at[3], 0: t}

    def exists(a, b):
        if a == 0:
            return has_y[b]
        if b == 0:
            return has_x[a]
        return has_x[a] & has_y[b]

    barrier = pltpu.get_barrier_semaphore()
    seam = slabs // 2
    greets = {1: (s < slabs - 1) & (s != seam - 1), -1: s == seam}
    greeted = {-1: (s > 0) & (s != seam), 1: s == seam - 1}
    per_side = 1 + jnp.where(has_y[1], 1, 0) + jnp.where(has_y[-1], 1, 0)

    def to_side(semaphore, sides):
        for a in (1, -1):
            for b in (0, 1, -1):

                @pl.when(sides[a] & has_y[b])
                def _():
                    pl.semaphore_signal(
                        semaphore,
                        inc=1,
                        device_id=(g, at_x[a], at_y[b]),
                        device_id_type=MESH,
                    )

    def from_side(sides):
        return per_side * (jnp.where(sides[1], 1, 0) + jnp.where(sides[-1], 1, 0))

    to_side(barrier, greets)
    for dg in range(2):
        for j in range(TILES):
            if dg + j > 0:
                pl.semaphore_signal(
                    barrier,
                    inc=1,
                    device_id=(other if dg else g, s, tile_at[j]),
                    device_id_type=MESH,
                )

    loads = [
        pltpu.make_async_copy(src, dst, in_sem.at[k])
        for k, (src, dst) in enumerate(
            [
                (site_hbm, site),
                (frac_hbm, frac),
                (shape_hbm, rest),
                (couple_hbm, couple),
                (pop_hbm.at[0], lat),
                (fluid_hbm.at[0], fluid),
            ]
        )
    ]
    for load in loads:
        load.start()

    payload[...] = jnp.zeros_like(payload)
    for load in loads[:3]:
        load.wait()
    site_value = site[...]
    coords = [
        site_value >> 10,
        (site_value >> 7) & (CY - 1),
        site_value & (NZ - 1),
    ]
    for d in range(3):
        offset = frac[d]
        position = f32(coords[d]) + offset
        centre = jnp.sum(position, axis=1, keepdims=True) * (1.0 / VERTS)
        push = -stiffness * (position - centre - rest[d])
        for c in range(CELLS):
            payload[c, d : d + 1, 0:VERTS] = offset[c : c + 1]
            payload[c, 4 + d : 5 + d, 0:VERTS] = push[c : c + 1]
    for c in range(CELLS):
        payload[c, 3:4, 0:VERTS] = f32(site_value[c : c + 1])

    owners = [owner_ref[c] for c in range(CELLS)]
    ranks = []
    for c in range(CELLS):
        rank = jnp.int32(0)
        for before in range(c):
            rank = rank + jnp.where(owners[before] == owners[c], 1, 0)
        ranks.append(rank)

    def chosen(j, k, c):
        return jnp.where((owners[c] == tile_at[j]) & (ranks[c] == k), 1.0, 0.0)

    for j in range(TILES):
        for k in range(CAP):
            slot = chosen(j, k, 0) * payload[0]
            for c in range(1, CELLS):
                slot = slot + chosen(j, k, c) * payload[c]
            cell_send[j, :, k * PAD : (k + 1) * PAD] = slot
            if j == 0:
                cell_recv[0, 0, :, k * PAD : (k + 1) * PAD] = slot

    def to_pair(src, dst, k):
        return pltpu.make_async_remote_copy(
            src_ref=src,
            dst_ref=dst,
            send_sem=pair_sems.at[0, k],
            recv_sem=pair_sems.at[1, k],
            device_id=(other, s, t),
            device_id_type=MESH,
        )

    loads[3].wait()
    loads[4].wait()
    row_0, row_1 = couple[0], couple[1]
    read_sites = row_0 + g * (row_1 - row_0)
    write_sites = row_1 + g * (row_0 - row_1)
    high, low = halves(lat[...].reshape(19 * XY, NZ))
    pop_half[:, 0:NZ] = high
    pop_half[:, NZ : 2 * NZ] = low
    chunk = 256
    for k in range(EDGE // chunk):
        sites = read_sites[:, k * chunk : (k + 1) * chunk]
        z_rows = lax.broadcasted_iota(jnp.int32, (NZ, chunk), 0)
        pick_z = jnp.where(z_rows == (sites & (NZ - 1)), 1.0, 0.0).astype(jnp.bfloat16)
        pick_z = jnp.concatenate([pick_z, pick_z], axis=0)
        xy_rows = lax.broadcasted_iota(jnp.int32, (XY, chunk), 0)
        pick_xy = jnp.where(xy_rows == (sites >> 7), 1.0, 0.0)
        found = dot_nn(pop_half[...], pick_z)
        for i in range(19):
            edge_send[i : i + 1, k * chunk : (k + 1) * chunk] = jnp.sum(
                found[i * XY : (i + 1) * XY] * pick_xy, axis=0, keepdims=True
            )
    rows = [edge_send[i : i + 1, :] for i in range(19)]
    density, momenta = moments(rows)
    target = equilibrium(density, [m / density for m in momenta])
    factor = jnp.where(window, 2.0 * tau_coarse / tau_fine, tau_fine / (2.0 * tau_coarse))
    for i in range(19):
        edge_send[i : i + 1, :] = target[i] + factor * (rows[i] - target[i])

    def hats(dg, j):
        cell = cell_recv[dg, j, 0:4]
        where_at = cell[3:4].astype(jnp.int32)
        z_rows = lax.broadcasted_iota(jnp.int32, (NZ, WIDE), 0) - (where_at & (NZ - 1))
        frac_z = cell[2:3]
        weight_z = jnp.where(z_rows == 0, 1.0 - frac_z, jnp.where(z_rows == 1, frac_z, 0.0))
        z_high, z_low = halves(weight_z)
        hat_z[dg, j, 0:NZ] = z_high
        hat_z[dg, j, NZ : 2 * NZ] = z_low
        y_rows = lax.broadcasted_iota(jnp.int32, (CY, WIDE), 0) - ((where_at >> 7) & (CY - 1))
        frac_y = cell[1:2]
        weight_y = jnp.where(y_rows == 0, 1.0 - frac_y, jnp.where(y_rows == 1, frac_y, 0.0))
        x_rows = lax.broadcasted_iota(jnp.int32, (CX, WIDE), 0) - (where_at >> 10)
        frac_x = cell[0:1]
        weight_x = jnp.where(x_rows == 0, 1.0 - frac_x, jnp.where(x_rows == 1, frac_x, 0.0))
        for x in range(CX):
            hat_xy[dg, j, x * CY : (x + 1) * CY] = weight_x[x : x + 1] * weight_y

    def spread(dg, j):
        hats(dg, j)
        weight_xy = hat_xy[dg, j]
        cell = cell_recv[dg, j]
        pushed = jnp.concatenate([weight_xy * cell[4 + d : 5 + d] for d in range(3)], axis=0)
        push_high, push_low = halves(pushed)
        both = dot_nt(jnp.concatenate([push_high, push_low], axis=0), hat_z[dg, j])
        high_rows, low_rows = both[0 : 3 * XY], both[3 * XY :]
        return high_rows[:, 0:NZ] + high_rows[:, NZ : 2 * NZ] + low_rows[:, 0:NZ]

    pl.semaphore_wait(barrier, 2 * TILES - 1 + from_side(greeted))

    edge_copy = to_pair(edge_send, edge_recv, 0)
    cell_copies = {
        (0, j): pltpu.make_async_remote_copy(
            src_ref=cell_send.at[j],
            dst_ref=cell_recv.at[0, j],
            send_sem=cell_sems.at[0, 0, j],
            recv_sem=cell_sems.at[1, 0, j],
            device_id=(g, s, tile_at[j]),
            device_id_type=MESH,
        )
        for j in (2, 1, 3)
    }
    for copy in cell_copies.values():
        copy.start()
    edge_copy.start()
    to_side(ready, greeted)
    late_copies = [
        pltpu.make_async_remote_copy(
            src_ref=cell_send.at[j, 0:4],
            dst_ref=cell_recv.at[1, j, 0:4],
            send_sem=cell_sems.at[0, 1, j],
            recv_sem=cell_sems.at[1, 1, j],
            device_id=(other, s, tile_at[j]),
            device_id_type=MESH,
        )
        for j in range(TILES)
    ]

    z_rows = lax.broadcasted_iota(jnp.int32, (NZ, EDGE), 0)
    put_z = jnp.where(z_rows == (write_sites & (NZ - 1)), 1.0, 0.0).astype(jnp.bfloat16)
    xy_rows = lax.broadcasted_iota(jnp.int32, (XY, EDGE), 0)
    put_xy = jnp.where(xy_rows == (write_sites >> 7), 1.0, 0.0)
    written = dot_nt(put_xy.astype(jnp.bfloat16), put_z).reshape(CX, CY, NZ) > 0.5
    total = spread(0, 0)
    for j in (1, 3, 2):
        cell_copies[0, j].wait_recv()
        total = total + spread(0, j)
    force_send[...] = total.reshape(3, CX, CY, NZ)
    force_copy = to_pair(force_send, force_recv, 2)
    force_copy.start()

    edge_copy.wait_recv()
    for i in range(19):
        row = edge_recv[i : i + 1, :]
        row_high = f32(row.astype(jnp.bfloat16))
        edge_high[i * XY : (i + 1) * XY] = (put_xy * row_high).astype(jnp.bfloat16)
        edge_low[i * XY : (i + 1) * XY] = (put_xy * (row - row_high)).astype(jnp.bfloat16)
    placed = dot_nt(edge_high[...], put_z) + dot_nt(edge_low[...], put_z)
    for i in range(19):
        new = placed[i * XY : (i + 1) * XY].reshape(CX, CY, NZ)
        lat[i] = jnp.where(written, new, lat[i])

    loads[5].wait()
    wet[...] = jnp.where(fluid[...] > 0, 1.0, 0.0)

    force_copy.wait_recv()
    for d in range(3):
        force[d] = force_send[d] + force_recv[d]

    @pl.when(g == 0)
    def _():
        for copy in late_copies:
            copy.start()

    relax = jnp.where(window, tau_fine, tau_coarse)
    inverse = jnp.where(window, 1.0 / tau_fine, 1.0 / tau_coarse)

    y_index = lax.broadcasted_iota(jnp.int32, (CX, CY, NZ), 1)
    z_index = lax.broadcasted_iota(jnp.int32, (CX, CY, NZ), 2)
    x_row = lax.broadcasted_iota(jnp.int32, (CX, NZ), 0)

    def shifted(block, move, low_x, high_x, low_y, high_y, corner):
        a, b, e = move
        if a == 1:
            block = jnp.concatenate([low_x[None], block[:-1]], axis=0)
        elif a == -1:
            block = jnp.concatenate([block[1:], high_x[None]], axis=0)
        if b != 0:
            side = low_y if b == 1 else high_y
            if a == 1:
                side = jnp.where(x_row == 0, corner, pltpu.roll(side, 1, 0))
            elif a == -1:
                side = jnp.where(x_row == CX - 1, corner, pltpu.roll(side, CX - 1, 0))
            block = pltpu.roll(block, 1 if b == 1 else CY - 1, 1)
            side = jnp.broadcast_to(side[:, None, :], (CX, CY, NZ))
            block = jnp.where(y_index == (0 if b == 1 else CY - 1), side, block)
        if e != 0:
            block = pltpu.roll(block, 1 if e == 1 else NZ - 1, 2)
        return block

    def halo_copies(turn):
        copies = []
        moves = [(1, 0), (-1, 0), (0, 1), (0, -1)]
        for k in range(4):
            copies.append(
                (
                    moves[k],
                    pltpu.make_async_remote_copy(
                        src_ref=face_send.at[turn, k],
                        dst_ref=face_recv.at[turn, k],
                        send_sem=face_sems.at[turn, 0, k],
                        recv_sem=face_sems.at[turn, 1, k],
                        device_id=(g, at_x[moves[k][0]], at_y[moves[k][1]]),
                        device_id_type=MESH,
                    ),
                )
            )
        for k, i in enumerate(DIAGONAL):
            a, b, _ = lattice_c[i]
            copies.append(
                (
                    (a, b),
                    pltpu.make_async_remote_copy(
                        src_ref=row_send.at[turn, k],
                        dst_ref=row_recv.at[turn, k],
                        send_sem=row_sems.at[turn, 0, k],
                        recv_sem=row_sems.at[turn, 1, k],
                        device_id=(g, at_x[a], at_y[b]),
                        device_id_type=MESH,
                    ),
                )
            )
        return copies

    def sweep(turn, meanwhile):
        popul = [lat[i] for i in range(19)]
        density, momenta = moments(popul)
        velocity = [(momenta[d] + relax * force[d]) / density for d in range(3)]
        target = equilibrium(density, velocity)
        wet_here = wet[...] > 0.5
        for i in range(19):
            post[i] = jnp.where(wet_here, popul[i] - (popul[i] - target[i]) * inverse, popul[i])
        for k in range(5):
            face_send[turn, 0, k] = post[X_UP[k], CX - 1]
            face_send[turn, 1, k] = post[X_DOWN[k], 0]
            face_send[turn, 2, k] = post[Y_UP[k], :, CY - 1, :]
            face_send[turn, 3, k] = post[Y_DOWN[k], :, 0, :]
        face_send[turn, 0, 5] = wet[CX - 1]
        face_send[turn, 1, 5] = wet[0]
        face_send[turn, 2, 5] = wet[:, CY - 1, :]
        face_send[turn, 3, 5] = wet[:, 0, :]
        for k, i in enumerate(DIAGONAL):
            x = CX - 1 if lattice_c[i][0] == 1 else 0
            y = CY - 1 if lattice_c[i][1] == 1 else 0
            row_send[turn, k, 0:1] = post[i, x, y : y + 1, :]
            row_send[turn, k, 1:2] = wet[x, y : y + 1, :]
        copies = halo_copies(turn)
        if turn == 0:

            @pl.when(greets[1] | greets[-1])
            def _():
                pl.semaphore_wait(ready, from_side(greets))

        for (a, b), copy in copies[4:] + copies[:4]:
            pl.when(exists(a, b))(copy.start)
        meanwhile()
        for (a, b), copy in copies:
            pl.when(exists(-a, -b))(copy.wait_recv)
        if turn == 0:
            ones = jnp.ones((8, NZ), jnp.int32)

            def known(flags, a, b):
                if a != 0:
                    flags = jnp.where(ones * s != (0 if a == 1 else slabs - 1), flags, 0.0)
                if b != 0:
                    flags = jnp.where(ones * t != (0 if b == 1 else TILES - 1), flags, 0.0)
                return flags

            for i in range(1, 19):
                a, b, e = lattice_c[i]
                corner = None
                if i in DIAGONAL:
                    k = DIAGONAL.index(i)
                    corner = known(jnp.broadcast_to(row_recv[0, k, 1:2], (8, NZ)), a, b)
                moved = shifted(
                    wet[...],
                    lattice_c[i],
                    known(face_recv[0, 0, 5], 1, 0),
                    known(face_recv[0, 1, 5], -1, 0),
                    known(face_recv[0, 2, 5], 0, 1),
                    known(face_recv[0, 3, 5], 0, -1),
                    corner,
                )
                if e != 0:
                    moved = jnp.where(z_index == (0 if e == 1 else NZ - 1), 0.0, moved)
                open_mask[i] = moved
        for i in range(19):
            if i == 0:
                lat[0] = post[0]
                continue
            a, b, e = lattice_c[i]
            moved = shifted(
                post[i],
                lattice_c[i],
                face_recv[turn, 0, X_UP.index(i)] if a == 1 else None,
                face_recv[turn, 1, X_DOWN.index(i)] if a == -1 else None,
                face_recv[turn, 2, Y_UP.index(i)] if b == 1 else None,
                face_recv[turn, 3, Y_DOWN.index(i)] if b == -1 else None,
                row_recv[turn, DIAGONAL.index(i), 0:1] if i in DIAGONAL else None,
            )
            moved = jnp.where(open_mask[i] > 0.5, moved, post[opposite[i]])
            lat[i] = jnp.where(wet_here, moved, post[i])

    def late_hats():
        for j in range(TILES):
            late_copies[j].wait_recv()
            hats(1, j)

    def half_velocity():
        density, momenta = moments([lat[i] for i in range(19)])
        for d in range(3):
            vel_send[d] = 0.5 * ((momenta[d] + 0.5 * force[d]) / density)

    sweep(0, lambda: None)
    vel_copy = to_pair(vel_send, vel_recv, 1)

    def return_copy(dg, j):
        return pltpu.make_async_remote_copy(
            src_ref=ret_send.at[dg, j],
            dst_ref=ret_recv.at[j],
            send_sem=ret_send_sems.at[dg, j],
            recv_sem=ret_recv_sems.at[j],
            device_id=(other if dg else g, s, tile_at[(TILES - j) % TILES]),
            device_id_type=MESH,
        )

    @pl.when(g == 0)
    def _():
        half_velocity()
        vel_copy.start()

    @pl.when(window)
    def _():
        sweep(1, late_hats)
        half_velocity()
        vel_copy.wait_recv()
        speed = (vel_send[...] + vel_recv[...]).reshape(3 * XY, NZ)
        speed_high, speed_low = halves(speed)
        speed_twice = jnp.concatenate([speed_high, speed_high], axis=1)
        for dg, j in ((1, 2), (1, 1), (1, 3), (0, 2), (1, 0), (0, 1), (0, 3), (0, 0)):
            seen = dot_nn(speed_twice, hat_z[dg, j]) + dot_nn(speed_low, hat_z[dg, j, 0:NZ])
            for d in range(3):
                reading = jnp.sum(
                    seen[d * XY : (d + 1) * XY] * hat_xy[dg, j], axis=0, keepdims=True
                )
                if dg + j > 0:
                    ret_send[dg, j, d : d + 1] = reading
                else:
                    ret_recv[0, d : d + 1] = reading
            if dg + j > 0:
                return_copy(dg, j).start()

    values = [None] * CELLS
    for j in (2, 1, 3, 0):
        if j > 0:
            return_copy(0, j).wait_recv()
        else:

            @pl.when(g == 0)
            def _():
                return_copy(1, 0).wait_recv()

        for c in range(CELLS):
            for k in range(CAP):
                term = chosen(j, k, c) * ret_recv[j, :, k * PAD : (k + 1) * PAD]
                values[c] = term if values[c] is None else values[c] + term
    for c in range(CELLS):
        for d in range(3):
            out_vel[d, c : c + 1] = values[c][d : d + 1, 0:VERTS]

    for (a, b), copy in halo_copies(0):
        pl.when(exists(a, b))(copy.wait_send)

    @pl.when(g == 0)
    def _():
        vel_copy.wait_send()
        for copy in late_copies:
            copy.wait_send()

    @pl.when(window)
    def _():
        for (a, b), copy in halo_copies(1):
            pl.when(exists(a, b))(copy.wait_send)
        for dg in range(2):
            for j in range(TILES):
                if dg + j > 0:
                    return_copy(dg, j).wait_send()

    for copy in cell_copies.values():
        copy.wait_send()
    edge_copy.wait_send()
    force_copy.wait_send()


def local(populations, fluid, couple, owner, vertex_site, frac, ref_shape):
    hbm = pl.BlockSpec(memory_space=pl.ANY)
    vmem = pl.BlockSpec(memory_space=pltpu.VMEM)
    real = jnp.float32
    half = jnp.bfloat16
    new, velocity = pl.pallas_call(
        kernel,
        out_shape=(
            pltpu.VMEM(populations.shape, real),
            pltpu.VMEM((3, CELLS, VERTS), real),
        ),
        in_specs=[hbm, hbm, hbm, pl.BlockSpec(memory_space=pltpu.SMEM), hbm, hbm, hbm],
        out_specs=(vmem, vmem),
        scratch_shapes=[
            pltpu.VMEM((CX, CY, NZ), jnp.int32),
            pltpu.VMEM((2, 1, EDGE), jnp.int32),
            pltpu.VMEM((CELLS, VERTS), jnp.int32),
            pltpu.VMEM((3, CELLS, VERTS), real),
            pltpu.VMEM((3, CELLS, VERTS), real),
            pltpu.VMEM((CELLS, 8, PAD), real),
            pltpu.VMEM((TILES, 8, WIDE), real),
            pltpu.VMEM((2, TILES, 8, WIDE), real),
            pltpu.VMEM((19 * XY, 2 * NZ), half),
            pltpu.VMEM((19, EDGE), real),
            pltpu.VMEM((19, EDGE), real),
            pltpu.VMEM((19 * XY, EDGE), half),
            pltpu.VMEM((19 * XY, EDGE), half),
            pltpu.VMEM((2, TILES, XY, WIDE), real),
            pltpu.VMEM((2, TILES, 2 * NZ, WIDE), half),
            pltpu.VMEM((3, CX, CY, NZ), real),
            pltpu.VMEM((3, CX, CY, NZ), real),
            pltpu.VMEM((3, CX, CY, NZ), real),
            pltpu.VMEM((19, CX, CY, NZ), real),
            pltpu.VMEM((CX, CY, NZ), real),
            pltpu.VMEM((19, CX, CY, NZ), real),
            pltpu.VMEM((2, 4, 6, 8, NZ), real),
            pltpu.VMEM((2, 4, 6, 8, NZ), real),
            pltpu.VMEM((2, 4, 2, NZ), real),
            pltpu.VMEM((2, 4, 2, NZ), real),
            pltpu.VMEM((3, CX, CY, NZ), real),
            pltpu.VMEM((3, CX, CY, NZ), real),
            pltpu.VMEM((2, TILES, 3, WIDE), real),
            pltpu.VMEM((TILES, 3, WIDE), real),
            pltpu.SemaphoreType.DMA((6,)),
            pltpu.SemaphoreType.DMA((2, 2, TILES)),
            pltpu.SemaphoreType.DMA((2, 3)),
            pltpu.SemaphoreType.DMA((2, 2, 4)),
            pltpu.SemaphoreType.DMA((2, 2, 4)),
            pltpu.SemaphoreType.DMA((2, TILES)),
            pltpu.SemaphoreType.DMA((TILES,)),
            pltpu.SemaphoreType.REGULAR,
        ],
        compiler_params=pltpu.CompilerParams(
            collective_id=0, has_side_effects=True, vmem_limit_bytes=62 * 2**20
        ),
    )(
        populations,
        fluid,
        couple.reshape(2, 1, EDGE),
        owner.reshape(CELLS),
        vertex_site,
        jnp.transpose(frac, (1, 0, 2)),
        jnp.transpose(ref_shape, (1, 0, 2)),
    )
    return new, jnp.transpose(velocity, (1, 0, 2))


def solution(mesh):
    return jax.shard_map(
        local,
        mesh=mesh,
        in_specs=(
            P("group", None, "slab", "tile", None),
            P("group", "slab", "tile", None),
            P("group", "slab", "tile", None),
            P(("group", "slab", "tile"), None),
            P(("group", "slab", "tile"), None),
            P(("group", "slab", "tile"), None, None),
            P(("group", "slab", "tile"), None, None),
        ),
        out_specs=(
            P("group", None, "slab", "tile", None),
            P(("group", "slab", "tile"), None, None),
        ),
        check_vma=False,
    )
```

```python
import jax
import jax.numpy as jnp
from jax import lax
from jax.experimental import pallas as pl
from jax.experimental.pallas import tpu as pltpu
from jax.sharding import PartitionSpec as P

MESH = pl.DeviceIdType.MESH
CX = 8
CY = 8
NZ = 128
XY = CX * CY
VERTS = 642
PAD = 768
WIDE = 2 * PAD
CELLS = 4
CAP = 2
EDGE = 1024
TILES = 4

lattice_c = [
    (0, 0, 0),
    (1, 0, 0),
    (-1, 0, 0),
    (0, 1, 0),
    (0, -1, 0),
    (0, 0, 1),
    (0, 0, -1),
    (1, 1, 0),
    (-1, -1, 0),
    (1, -1, 0),
    (-1, 1, 0),
    (1, 0, 1),
    (-1, 0, -1),
    (1, 0, -1),
    (-1, 0, 1),
    (0, 1, 1),
    (0, -1, -1),
    (0, 1, -1),
    (0, -1, 1),
]
lattice_w = [1.0 / 3.0] + [1.0 / 18.0] * 6 + [1.0 / 36.0] * 12
opposite = [0, 2, 1, 4, 3, 6, 5, 8, 7, 10, 9, 12, 11, 14, 13, 16, 15, 18, 17]
tau_coarse = 0.8
tau_fine = 1.1
stiffness = 0.01

X_UP = [i for i in range(19) if lattice_c[i][0] == 1]
X_DOWN = [i for i in range(19) if lattice_c[i][0] == -1]
Y_UP = [i for i in range(19) if lattice_c[i][1] == 1]
Y_DOWN = [i for i in range(19) if lattice_c[i][1] == -1]
DIAGONAL = [7, 8, 9, 10]


def f32(x):
    return x.astype(jnp.float32)


def halves(x):
    high = x.astype(jnp.bfloat16)
    low = (x - f32(high)).astype(jnp.bfloat16)
    return high, low


def dot_nn(a, b):
    return lax.dot_general(a, b, (((1,), (0,)), ((), ())), preferred_element_type=jnp.float32)


def dot_nt(a, b):
    return lax.dot_general(a, b, (((1,), (1,)), ((), ())), preferred_element_type=jnp.float32)


def moments(popul):
    density = popul[0]
    momenta = [None, None, None]
    for i in range(1, 19):
        density = density + popul[i]
        for d in range(3):
            sign = lattice_c[i][d]
            if sign == 0:
                continue
            if momenta[d] is None:
                momenta[d] = popul[i]
            elif sign > 0:
                momenta[d] = momenta[d] + popul[i]
            else:
                momenta[d] = momenta[d] - popul[i]
    return density, momenta


def equilibrium(density, velocity):
    ux, uy, uz = velocity
    base = 1.0 - 1.5 * (ux * ux + uy * uy + uz * uz)
    terms = [None] * 19
    terms[0] = lattice_w[0] * density * base
    for i in range(1, 19, 2):
        along = None
        for d in range(3):
            sign = lattice_c[i][d]
            if sign == 0:
                continue
            if along is None:
                along = velocity[d]
            elif sign > 0:
                along = along + velocity[d]
            else:
                along = along - velocity[d]
        weight = lattice_w[i] * density
        even = base + 4.5 * along * along
        odd = 3.0 * along
        terms[i] = weight * (even + odd)
        terms[i + 1] = weight * (even - odd)
    return terms


def kernel(
    pop_hbm,
    fluid_hbm,
    couple_hbm,
    owner_ref,
    site_hbm,
    frac_hbm,
    shape_hbm,
    out_pop,
    out_vel,
    fluid,
    couple,
    site,
    frac,
    rest,
    payload,
    cell_send,
    cell_recv,
    pop_half,
    edge_send,
    edge_recv,
    edge_high,
    edge_low,
    hat_xy,
    hat_z,
    force_send,
    force_recv,
    force,
    post,
    wet,
    open_mask,
    face_send,
    face_recv,
    row_send,
    row_recv,
    vel_send,
    vel_recv,
    ret_send,
    ret_recv,
    in_sem,
    cell_sems,
    pair_sems,
    face_sems,
    row_sems,
    ret_send_sems,
    ret_recv_sems,
    ready,
):
    lat = out_pop.at[0]
    g = lax.axis_index("group")
    s = lax.axis_index("slab")
    t = lax.axis_index("tile")
    slabs = lax.axis_size("slab")
    window = g == 1
    up_s, down_s = lax.rem(s + 1, slabs), lax.rem(s + slabs - 1, slabs)
    tile_at = [lax.rem(t + j, TILES) for j in range(TILES)]
    other = 1 - g
    has_x = {1: s < slabs - 1, -1: s > 0}
    has_y = {1: t < TILES - 1, -1: t > 0, 0: t >= 0}
    at_x = {1: up_s, -1: down_s, 0: s}
    at_y = {1: tile_at[1], -1: tile_at[3], 0: t}

    def exists(a, b):
        if a == 0:
            return has_y[b]
        if b == 0:
            return has_x[a]
        return has_x[a] & has_y[b]

    barrier = pltpu.get_barrier_semaphore()
    seam = slabs // 2
    greets = {1: (s < slabs - 1) & (s != seam - 1), -1: s == seam}
    greeted = {-1: (s > 0) & (s != seam), 1: s == seam - 1}
    per_side = 1 + jnp.where(has_y[1], 1, 0) + jnp.where(has_y[-1], 1, 0)

    def to_side(semaphore, sides):
        for a in (1, -1):
            for b in (0, 1, -1):

                @pl.when(sides[a] & has_y[b])
                def _():
                    pl.semaphore_signal(
                        semaphore,
                        inc=1,
                        device_id=(g, at_x[a], at_y[b]),
                        device_id_type=MESH,
                    )

    def from_side(sides):
        return per_side * (jnp.where(sides[1], 1, 0) + jnp.where(sides[-1], 1, 0))

    to_side(barrier, greets)
    for dg in range(2):
        for j in range(TILES):
            if dg + j > 0:
                pl.semaphore_signal(
                    barrier,
                    inc=1,
                    device_id=(other if dg else g, s, tile_at[j]),
                    device_id_type=MESH,
                )

    loads = [
        pltpu.make_async_copy(src, dst, in_sem.at[k])
        for k, (src, dst) in enumerate(
            [
                (site_hbm, site),
                (frac_hbm, frac),
                (shape_hbm, rest),
                (couple_hbm, couple),
                (pop_hbm.at[0], lat),
                (fluid_hbm.at[0], fluid),
            ]
        )
    ]
    for load in loads:
        load.start()

    payload[...] = jnp.zeros_like(payload)
    for load in loads[:3]:
        load.wait()
    site_value = site[...]
    coords = [
        site_value >> 10,
        (site_value >> 7) & (CY - 1),
        site_value & (NZ - 1),
    ]
    for d in range(3):
        offset = frac[d]
        position = f32(coords[d]) + offset
        centre = jnp.sum(position, axis=1, keepdims=True) * (1.0 / VERTS)
        push = -stiffness * (position - centre - rest[d])
        for c in range(CELLS):
            payload[c, d : d + 1, 0:VERTS] = offset[c : c + 1]
            payload[c, 4 + d : 5 + d, 0:VERTS] = push[c : c + 1]
    for c in range(CELLS):
        payload[c, 3:4, 0:VERTS] = f32(site_value[c : c + 1])

    owners = [owner_ref[c] for c in range(CELLS)]
    ranks = []
    for c in range(CELLS):
        rank = jnp.int32(0)
        for before in range(c):
            rank = rank + jnp.where(owners[before] == owners[c], 1, 0)
        ranks.append(rank)

    def chosen(j, k, c):
        return jnp.where((owners[c] == tile_at[j]) & (ranks[c] == k), 1.0, 0.0)

    for j in range(TILES):
        for k in range(CAP):
            slot = chosen(j, k, 0) * payload[0]
            for c in range(1, CELLS):
                slot = slot + chosen(j, k, c) * payload[c]
            cell_send[j, :, k * PAD : (k + 1) * PAD] = slot
            if j == 0:
                cell_recv[0, 0, :, k * PAD : (k + 1) * PAD] = slot

    def to_pair(src, dst, k):
        return pltpu.make_async_remote_copy(
            src_ref=src,
            dst_ref=dst,
            send_sem=pair_sems.at[0, k],
            recv_sem=pair_sems.at[1, k],
            device_id=(other, s, t),
            device_id_type=MESH,
        )

    loads[3].wait()
    loads[4].wait()
    row_0, row_1 = couple[0], couple[1]
    read_sites = row_0 + g * (row_1 - row_0)
    write_sites = row_1 + g * (row_0 - row_1)
    high, low = halves(lat[...].reshape(19 * XY, NZ))
    pop_half[:, 0:NZ] = high
    pop_half[:, NZ : 2 * NZ] = low
    chunk = 256
    for k in range(EDGE // chunk):
        sites = read_sites[:, k * chunk : (k + 1) * chunk]
        z_rows = lax.broadcasted_iota(jnp.int32, (NZ, chunk), 0)
        pick_z = jnp.where(z_rows == (sites & (NZ - 1)), 1.0, 0.0).astype(jnp.bfloat16)
        pick_z = jnp.concatenate([pick_z, pick_z], axis=0)
        xy_rows = lax.broadcasted_iota(jnp.int32, (XY, chunk), 0)
        pick_xy = jnp.where(xy_rows == (sites >> 7), 1.0, 0.0)
        found = dot_nn(pop_half[...], pick_z)
        for i in range(19):
            edge_send[i : i + 1, k * chunk : (k + 1) * chunk] = jnp.sum(
                found[i * XY : (i + 1) * XY] * pick_xy, axis=0, keepdims=True
            )
    rows = [edge_send[i : i + 1, :] for i in range(19)]
    density, momenta = moments(rows)
    target = equilibrium(density, [m / density for m in momenta])
    factor = jnp.where(window, 2.0 * tau_coarse / tau_fine, tau_fine / (2.0 * tau_coarse))
    for i in range(19):
        edge_send[i : i + 1, :] = target[i] + factor * (rows[i] - target[i])

    def hats(dg, j):
        cell = cell_recv[dg, j, 0:4]
        where_at = cell[3:4].astype(jnp.int32)
        z_rows = lax.broadcasted_iota(jnp.int32, (NZ, WIDE), 0) - (where_at & (NZ - 1))
        frac_z = cell[2:3]
        weight_z = jnp.where(z_rows == 0, 1.0 - frac_z, jnp.where(z_rows == 1, frac_z, 0.0))
        z_high, z_low = halves(weight_z)
        hat_z[dg, j, 0:NZ] = z_high
        hat_z[dg, j, NZ : 2 * NZ] = z_low
        y_rows = lax.broadcasted_iota(jnp.int32, (CY, WIDE), 0) - ((where_at >> 7) & (CY - 1))
        frac_y = cell[1:2]
        weight_y = jnp.where(y_rows == 0, 1.0 - frac_y, jnp.where(y_rows == 1, frac_y, 0.0))
        x_rows = lax.broadcasted_iota(jnp.int32, (CX, WIDE), 0) - (where_at >> 10)
        frac_x = cell[0:1]
        weight_x = jnp.where(x_rows == 0, 1.0 - frac_x, jnp.where(x_rows == 1, frac_x, 0.0))
        for x in range(CX):
            hat_xy[dg, j, x * CY : (x + 1) * CY] = weight_x[x : x + 1] * weight_y

    def spread(dg, j):
        hats(dg, j)
        weight_xy = hat_xy[dg, j]
        cell = cell_recv[dg, j]
        pushed = jnp.concatenate([weight_xy * cell[4 + d : 5 + d] for d in range(3)], axis=0)
        push_high, push_low = halves(pushed)
        both = dot_nt(jnp.concatenate([push_high, push_low], axis=0), hat_z[dg, j])
        high_rows, low_rows = both[0 : 3 * XY], both[3 * XY :]
        return high_rows[:, 0:NZ] + high_rows[:, NZ : 2 * NZ] + low_rows[:, 0:NZ]

    pl.semaphore_wait(barrier, 2 * TILES - 1 + from_side(greeted))

    edge_copy = to_pair(edge_send, edge_recv, 0)
    cell_copies = {
        (0, j): pltpu.make_async_remote_copy(
            src_ref=cell_send.at[j],
            dst_ref=cell_recv.at[0, j],
            send_sem=cell_sems.at[0, 0, j],
            recv_sem=cell_sems.at[1, 0, j],
            device_id=(g, s, tile_at[j]),
            device_id_type=MESH,
        )
        for j in (2, 1, 3)
    }
    for copy in cell_copies.values():
        copy.start()
    edge_copy.start()
    to_side(ready, greeted)
    late_copies = [
        pltpu.make_async_remote_copy(
            src_ref=cell_send.at[j, 0:4],
            dst_ref=cell_recv.at[1, j, 0:4],
            send_sem=cell_sems.at[0, 1, j],
            recv_sem=cell_sems.at[1, 1, j],
            device_id=(other, s, tile_at[j]),
            device_id_type=MESH,
        )
        for j in range(TILES)
    ]

    z_rows = lax.broadcasted_iota(jnp.int32, (NZ, EDGE), 0)
    put_z = jnp.where(z_rows == (write_sites & (NZ - 1)), 1.0, 0.0).astype(jnp.bfloat16)
    xy_rows = lax.broadcasted_iota(jnp.int32, (XY, EDGE), 0)
    put_xy = jnp.where(xy_rows == (write_sites >> 7), 1.0, 0.0)
    written = dot_nt(put_xy.astype(jnp.bfloat16), put_z).reshape(CX, CY, NZ) > 0.5
    total = spread(0, 0)
    for j in (1, 3, 2):
        cell_copies[0, j].wait_recv()
        total = total + spread(0, j)
    force_send[...] = total.reshape(3, CX, CY, NZ)
    force_copy = to_pair(force_send, force_recv, 2)
    force_copy.start()

    edge_copy.wait_recv()
    for i in range(19):
        row = edge_recv[i : i + 1, :]
        row_high = f32(row.astype(jnp.bfloat16))
        edge_high[i * XY : (i + 1) * XY] = (put_xy * row_high).astype(jnp.bfloat16)
        edge_low[i * XY : (i + 1) * XY] = (put_xy * (row - row_high)).astype(jnp.bfloat16)
    placed = dot_nt(edge_high[...], put_z) + dot_nt(edge_low[...], put_z)
    for i in range(19):
        new = placed[i * XY : (i + 1) * XY].reshape(CX, CY, NZ)
        lat[i] = jnp.where(written, new, lat[i])

    loads[5].wait()
    wet[...] = jnp.where(fluid[...] > 0, 1.0, 0.0)

    force_copy.wait_recv()
    for d in range(3):
        force[d] = force_send[d] + force_recv[d]

    @pl.when(g == 0)
    def _():
        for copy in late_copies:
            copy.start()

    relax = jnp.where(window, tau_fine, tau_coarse)
    inverse = jnp.where(window, 1.0 / tau_fine, 1.0 / tau_coarse)

    y_index = lax.broadcasted_iota(jnp.int32, (CX, CY, NZ), 1)
    z_index = lax.broadcasted_iota(jnp.int32, (CX, CY, NZ), 2)
    x_row = lax.broadcasted_iota(jnp.int32, (CX, NZ), 0)

    def shifted(block, move, low_x, high_x, low_y, high_y, corner):
        a, b, e = move
        if a == 1:
            block = jnp.concatenate([low_x[None], block[:-1]], axis=0)
        elif a == -1:
            block = jnp.concatenate([block[1:], high_x[None]], axis=0)
        if b != 0:
            side = low_y if b == 1 else high_y
            if a == 1:
                side = jnp.where(x_row == 0, corner, pltpu.roll(side, 1, 0))
            elif a == -1:
                side = jnp.where(x_row == CX - 1, corner, pltpu.roll(side, CX - 1, 0))
            block = pltpu.roll(block, 1 if b == 1 else CY - 1, 1)
            side = jnp.broadcast_to(side[:, None, :], (CX, CY, NZ))
            block = jnp.where(y_index == (0 if b == 1 else CY - 1), side, block)
        if e != 0:
            block = pltpu.roll(block, 1 if e == 1 else NZ - 1, 2)
        return block

    def halo_copies(turn):
        copies = []
        moves = [(1, 0), (-1, 0), (0, 1), (0, -1)]
        for k in range(4):
            copies.append(
                (
                    moves[k],
                    pltpu.make_async_remote_copy(
                        src_ref=face_send.at[turn, k, 0 : 6 - turn],
                        dst_ref=face_recv.at[turn, k, 0 : 6 - turn],
                        send_sem=face_sems.at[turn, 0, k],
                        recv_sem=face_sems.at[turn, 1, k],
                        device_id=(g, at_x[moves[k][0]], at_y[moves[k][1]]),
                        device_id_type=MESH,
                    ),
                )
            )
        for k, i in enumerate(DIAGONAL):
            a, b, _ = lattice_c[i]
            copies.append(
                (
                    (a, b),
                    pltpu.make_async_remote_copy(
                        src_ref=row_send.at[turn, k],
                        dst_ref=row_recv.at[turn, k],
                        send_sem=row_sems.at[turn, 0, k],
                        recv_sem=row_sems.at[turn, 1, k],
                        device_id=(g, at_x[a], at_y[b]),
                        device_id_type=MESH,
                    ),
                )
            )
        return copies

    def sweep(turn, meanwhile):
        popul = [lat[i] for i in range(19)]
        density, momenta = moments(popul)
        velocity = [(momenta[d] + relax * force[d]) / density for d in range(3)]
        target = equilibrium(density, velocity)
        wet_here = wet[...] > 0.5
        for i in range(19):
            post[i] = jnp.where(wet_here, popul[i] - (popul[i] - target[i]) * inverse, popul[i])
        for k in range(5):
            face_send[turn, 0, k] = post[X_UP[k], CX - 1]
            face_send[turn, 1, k] = post[X_DOWN[k], 0]
            face_send[turn, 2, k] = post[Y_UP[k], :, CY - 1, :]
            face_send[turn, 3, k] = post[Y_DOWN[k], :, 0, :]
        face_send[turn, 0, 5] = wet[CX - 1]
        face_send[turn, 1, 5] = wet[0]
        face_send[turn, 2, 5] = wet[:, CY - 1, :]
        face_send[turn, 3, 5] = wet[:, 0, :]
        for k, i in enumerate(DIAGONAL):
            x = CX - 1 if lattice_c[i][0] == 1 else 0
            y = CY - 1 if lattice_c[i][1] == 1 else 0
            row_send[turn, k, 0:1] = post[i, x, y : y + 1, :]
            row_send[turn, k, 1:2] = wet[x, y : y + 1, :]
        copies = halo_copies(turn)
        if turn == 0:

            @pl.when(greets[1] | greets[-1])
            def _():
                pl.semaphore_wait(ready, from_side(greets))

        for (a, b), copy in copies[4:] + copies[:4]:
            pl.when(exists(a, b))(copy.start)
        meanwhile()
        for (a, b), copy in copies:
            pl.when(exists(-a, -b))(copy.wait_recv)
        if turn == 0:
            ones = jnp.ones((8, NZ), jnp.int32)

            def known(flags, a, b):
                if a != 0:
                    flags = jnp.where(ones * s != (0 if a == 1 else slabs - 1), flags, 0.0)
                if b != 0:
                    flags = jnp.where(ones * t != (0 if b == 1 else TILES - 1), flags, 0.0)
                return flags

            for i in range(1, 19):
                a, b, e = lattice_c[i]
                corner = None
                if i in DIAGONAL:
                    k = DIAGONAL.index(i)
                    corner = known(jnp.broadcast_to(row_recv[0, k, 1:2], (8, NZ)), a, b)
                moved = shifted(
                    wet[...],
                    lattice_c[i],
                    known(face_recv[0, 0, 5], 1, 0),
                    known(face_recv[0, 1, 5], -1, 0),
                    known(face_recv[0, 2, 5], 0, 1),
                    known(face_recv[0, 3, 5], 0, -1),
                    corner,
                )
                if e != 0:
                    moved = jnp.where(z_index == (0 if e == 1 else NZ - 1), 0.0, moved)
                open_mask[i] = moved
        for i in range(19):
            if i == 0:
                lat[0] = post[0]
                continue
            a, b, e = lattice_c[i]
            moved = shifted(
                post[i],
                lattice_c[i],
                face_recv[turn, 0, X_UP.index(i)] if a == 1 else None,
                face_recv[turn, 1, X_DOWN.index(i)] if a == -1 else None,
                face_recv[turn, 2, Y_UP.index(i)] if b == 1 else None,
                face_recv[turn, 3, Y_DOWN.index(i)] if b == -1 else None,
                row_recv[turn, DIAGONAL.index(i), 0:1] if i in DIAGONAL else None,
            )
            moved = jnp.where(open_mask[i] > 0.5, moved, post[opposite[i]])
            lat[i] = jnp.where(wet_here, moved, post[i])

    def late_hats():
        for j in range(TILES):
            late_copies[j].wait_recv()
            hats(1, j)

    def half_velocity():
        density, momenta = moments([lat[i] for i in range(19)])
        for d in range(3):
            vel_send[d] = 0.5 * ((momenta[d] + 0.5 * force[d]) / density)

    sweep(0, lambda: None)
    vel_copy = to_pair(vel_send, vel_recv, 1)

    def return_copy(dg, j):
        return pltpu.make_async_remote_copy(
            src_ref=ret_send.at[dg, j],
            dst_ref=ret_recv.at[j],
            send_sem=ret_send_sems.at[dg, j],
            recv_sem=ret_recv_sems.at[j],
            device_id=(other if dg else g, s, tile_at[(TILES - j) % TILES]),
            device_id_type=MESH,
        )

    @pl.when(g == 0)
    def _():
        half_velocity()
        vel_copy.start()

    @pl.when(window)
    def _():
        sweep(1, late_hats)
        half_velocity()
        vel_copy.wait_recv()
        speed = (vel_send[...] + vel_recv[...]).reshape(3 * XY, NZ)
        speed_high, speed_low = halves(speed)
        speed_twice = jnp.concatenate([speed_high, speed_high], axis=1)
        for dg, j in ((1, 2), (1, 1), (1, 3), (0, 2), (1, 0), (0, 1), (0, 3), (0, 0)):
            seen = dot_nn(speed_twice, hat_z[dg, j]) + dot_nn(speed_low, hat_z[dg, j, 0:NZ])
            for d in range(3):
                reading = jnp.sum(
                    seen[d * XY : (d + 1) * XY] * hat_xy[dg, j], axis=0, keepdims=True
                )
                if dg + j > 0:
                    ret_send[dg, j, d : d + 1] = reading
                else:
                    ret_recv[0, d : d + 1] = reading
            if dg + j > 0:
                return_copy(dg, j).start()

    values = [None] * CELLS
    for j in (2, 1, 3, 0):
        if j > 0:
            return_copy(0, j).wait_recv()
        else:

            @pl.when(g == 0)
            def _():
                return_copy(1, 0).wait_recv()

        for c in range(CELLS):
            for k in range(CAP):
                term = chosen(j, k, c) * ret_recv[j, :, k * PAD : (k + 1) * PAD]
                values[c] = term if values[c] is None else values[c] + term
    for c in range(CELLS):
        for d in range(3):
            out_vel[d, c : c + 1] = values[c][d : d + 1, 0:VERTS]

    for (a, b), copy in halo_copies(0):
        pl.when(exists(a, b))(copy.wait_send)

    @pl.when(g == 0)
    def _():
        vel_copy.wait_send()
        for copy in late_copies:
            copy.wait_send()

    @pl.when(window)
    def _():
        for (a, b), copy in halo_copies(1):
            pl.when(exists(a, b))(copy.wait_send)
        for dg in range(2):
            for j in range(TILES):
                if dg + j > 0:
                    return_copy(dg, j).wait_send()

    for copy in cell_copies.values():
        copy.wait_send()
    edge_copy.wait_send()
    force_copy.wait_send()


def local(populations, fluid, couple, owner, vertex_site, frac, ref_shape):
    hbm = pl.BlockSpec(memory_space=pl.ANY)
    vmem = pl.BlockSpec(memory_space=pltpu.VMEM)
    real = jnp.float32
    half = jnp.bfloat16
    new, velocity = pl.pallas_call(
        kernel,
        out_shape=(
            pltpu.VMEM(populations.shape, real),
            pltpu.VMEM((3, CELLS, VERTS), real),
        ),
        in_specs=[hbm, hbm, hbm, pl.BlockSpec(memory_space=pltpu.SMEM), hbm, hbm, hbm],
        out_specs=(vmem, vmem),
        scratch_shapes=[
            pltpu.VMEM((CX, CY, NZ), jnp.int32),
            pltpu.VMEM((2, 1, EDGE), jnp.int32),
            pltpu.VMEM((CELLS, VERTS), jnp.int32),
            pltpu.VMEM((3, CELLS, VERTS), real),
            pltpu.VMEM((3, CELLS, VERTS), real),
            pltpu.VMEM((CELLS, 8, PAD), real),
            pltpu.VMEM((TILES, 8, WIDE), real),
            pltpu.VMEM((2, TILES, 8, WIDE), real),
            pltpu.VMEM((19 * XY, 2 * NZ), half),
            pltpu.VMEM((19, EDGE), real),
            pltpu.VMEM((19, EDGE), real),
            pltpu.VMEM((19 * XY, EDGE), half),
            pltpu.VMEM((19 * XY, EDGE), half),
            pltpu.VMEM((2, TILES, XY, WIDE), real),
            pltpu.VMEM((2, TILES, 2 * NZ, WIDE), half),
            pltpu.VMEM((3, CX, CY, NZ), real),
            pltpu.VMEM((3, CX, CY, NZ), real),
            pltpu.VMEM((3, CX, CY, NZ), real),
            pltpu.VMEM((19, CX, CY, NZ), real),
            pltpu.VMEM((CX, CY, NZ), real),
            pltpu.VMEM((19, CX, CY, NZ), real),
            pltpu.VMEM((2, 4, 6, 8, NZ), real),
            pltpu.VMEM((2, 4, 6, 8, NZ), real),
            pltpu.VMEM((2, 4, 2, NZ), real),
            pltpu.VMEM((2, 4, 2, NZ), real),
            pltpu.VMEM((3, CX, CY, NZ), real),
            pltpu.VMEM((3, CX, CY, NZ), real),
            pltpu.VMEM((2, TILES, 3, WIDE), real),
            pltpu.VMEM((TILES, 3, WIDE), real),
            pltpu.SemaphoreType.DMA((6,)),
            pltpu.SemaphoreType.DMA((2, 2, TILES)),
            pltpu.SemaphoreType.DMA((2, 3)),
            pltpu.SemaphoreType.DMA((2, 2, 4)),
            pltpu.SemaphoreType.DMA((2, 2, 4)),
            pltpu.SemaphoreType.DMA((2, TILES)),
            pltpu.SemaphoreType.DMA((TILES,)),
            pltpu.SemaphoreType.REGULAR,
        ],
        compiler_params=pltpu.CompilerParams(
            collective_id=0, has_side_effects=True, vmem_limit_bytes=62 * 2**20
        ),
    )(
        populations,
        fluid,
        couple.reshape(2, 1, EDGE),
        owner.reshape(CELLS),
        vertex_site,
        jnp.transpose(frac, (1, 0, 2)),
        jnp.transpose(ref_shape, (1, 0, 2)),
    )
    return new, jnp.transpose(velocity, (1, 0, 2))


def solution(mesh):
    return jax.shard_map(
        local,
        mesh=mesh,
        in_specs=(
            P("group", None, "slab", "tile", None),
            P("group", "slab", "tile", None),
            P("group", "slab", "tile", None),
            P(("group", "slab", "tile"), None),
            P(("group", "slab", "tile"), None),
            P(("group", "slab", "tile"), None, None),
            P(("group", "slab", "tile"), None, None),
        ),
        out_specs=(
            P("group", None, "slab", "tile", None),
            P(("group", "slab", "tile"), None, None),
        ),
        check_vma=False,
    )
```
